256 devices in a mesh: tok: 16 (over x, z_hi, core), ch: 16 (over y, z_lo).
Axes of the slice: x: 4, y: 4, z: 8 (z_hi: 2, z_lo: 4; z = z_hi * 4 + z_lo), core: 2. Of those that a mesh axis runs over, the one named last changes fastest.
Arguments:
- tokens: bfloat16 [6144, 8192], P('tok', 'ch'), may hold values from -6 to 6
- value_weight: bfloat16 [8192, 8192], P('tok', 'ch'), may hold values from -0.0625 to 0.0625
- key_gate: bfloat16 [6144, 8192], P('tok', 'ch'), may hold values from -6 to 6
- query_gate: bfloat16 [6144, 8192], P('tok', 'ch'), may hold values from -6 to 6
- conv_filter: float32 [512, 128], P('ch'), may hold values from -0.5 to 0.5
- out_weight: bfloat16 [8192, 8192], P('tok', 'ch'), may hold values from -0.0625 to 0.0625
Outputs:
- mixed: bfloat16 [6144, 8192], P('tok', 'ch')
The draws below stay inside these ranges and needn't reach their ends.
All inputs are finite; a program needn't handle non-finite values.
Results may differ from the reference program's by a relative error of at most 0.02.
Values may be sent and summed in bfloat16 or wider, within the bound.
A program may use at most 64 MiB of HBM per device.

```python
import jax
import jax.numpy as jnp
from jax import lax

D = 8192
TAPS = 128
GROUP = 16
TOKENS = 6144
GROUPS = 512


def steps_of(rng, shape, split, least, top_value):
    gain = 1.0
    for dim, blocks in split:
        heights = jax.random.uniform(jax.random.fold_in(jax.random.fold_in(rng, 6), dim), (blocks,), jnp.float32, least / len(split), top_value / len(split))
        gain = gain * jnp.repeat(jnp.exp(heights), shape[dim] // blocks).reshape((-1,) + (1,) * (len(shape) - 1 - dim))
    return gain


def centred(stream_key, extent, width, most, shards=(), kind=jnp.bfloat16):
    values = jax.random.normal(stream_key, extent, jnp.float32) * width
    if len(shards) > 0:
        values = steps_of(stream_key, extent, shards, -0.22, 0.18) * values
    return jnp.clip(values, min=-most, max=most).astype(kind)


def setup_inputs(seed: int = 0) -> dict:
    seeds = jax.random.split(jax.random.key(seed), 7)
    return {
        "tokens": centred(seeds[0], (TOKENS, D), 1.0, 6.0, ((0, 16), (1, 16))),
        "value_weight": centred(seeds[1], (D, D), D ** -0.5, 0.0625, ((0, 16), (1, 16))),
        "key_gate": centred(seeds[2], (TOKENS, D), 1.0, 6.0, ((0, 16), (1, 16))),
        "query_gate": centred(seeds[3], (TOKENS, D), 1.0, 6.0, ((0, 16), (1, 16))),
        "conv_filter": centred(seeds[4], (GROUPS, TAPS), TAPS ** -0.5, 0.5, ((0, 16),), jnp.float32),
        "out_weight": centred(seeds[5], (D, D), D ** -0.5, 0.0625, ((0, 16), (1, 16))),
    }


def reference(tokens, value_weight, key_gate, query_gate, conv_filter, out_weight):
    values = jnp.dot(tokens, value_weight, preferred_element_type=jnp.float32).astype(jnp.bfloat16)
    gated = (values.astype(jnp.float32) * key_gate.astype(jnp.float32)).astype(jnp.bfloat16)
    per_channel = jnp.repeat(conv_filter, GROUP, axis=0)
    padded = jnp.pad(gated.astype(jnp.float32), ((TAPS - 1, 0), (0, 0)))

    def add_tap(tap, total):
        window = lax.dynamic_slice_in_dim(padded, (TAPS - 1 - tap).astype(jnp.int32), TOKENS, 0)
        coeff = lax.dynamic_slice_in_dim(per_channel, tap.astype(jnp.int32), 1, 1)[:, 0]
        return total + window * coeff[None, :]

    conv = lax.fori_loop(jnp.int32(0), jnp.int32(TAPS), add_tap, jnp.zeros((TOKENS, D), jnp.float32))
    shaped = (conv * query_gate.astype(jnp.float32)).astype(jnp.bfloat16)
    return jnp.dot(shaped, out_weight, preferred_element_type=jnp.float32).astype(jnp.bfloat16)
```

```python
import functools

import jax
import jax.numpy as jnp
from jax import lax
from jax.experimental import pallas as pl
from jax.experimental.pallas import tpu as pltpu
from jax.sharding import PartitionSpec as P

MESH = pl.DeviceIdType.MESH
TAPS = 128
GROUP = 16
ROWS = 384
WIDTH = 512
RELAY = 16
WHOLE = ((0, 384),)
PARTS = ((128, 256), (0, 128))


class Names:
    def __init__(self):
        self.index = {}

    def __call__(self, name):
        return self.index.setdefault(name, len(self.index))


def place(x, y, z, c):
    return (x * 4 + (z // 4) * 2 + c, y * 4 + lax.rem(z, 4))


def kernel(
    tok_hbm, wv_hbm, key_hbm, query_hbm, filt_ref, wo_hbm,
    out_ref,
    wbuf_v, wbuf_o, tbuf_v, tbuf_o, band, base, ext, key, query,
    acc_away, acc_own, part_out, part_in, send_sem, recv_sem, local_sem,
):
    tok = lax.axis_index("tok")
    ch = lax.axis_index("ch")
    x, zh, c = tok // 4, lax.rem(tok // 2, 2), lax.rem(tok, 2)
    y, zl = ch // 4, lax.rem(ch, 4)
    zl1, zl0 = zl // 2, lax.rem(zl, 2)
    z = zh * 4 + zl
    master = c == zl0
    nm = jnp.logical_not(master)

    def near(zl0_):
        return zh * 4 + zl1 * 2 + zl0_

    xp, xm, x2 = lax.rem(x + 1, 4), lax.rem(x + 3, 4), lax.rem(x + 2, 4)
    yp, ym, y2 = lax.rem(y + 1, 4), lax.rem(y + 3, 4), lax.rem(y + 2, 4)
    dev_xp, dev_xm = place(xp, y, z, c), place(xm, y, z, c)
    dev_yp, dev_ym = place(x, yp, z, c), place(x, ym, z, c)
    dev_z1 = place(x, y, near(1 - zl0), c)
    dev_z2 = place(x, y, zh * 4 + (1 - zl1) * 2 + zl0, c)
    far_zl0 = jnp.where(master, zl0, 1 - zl0)
    dev_far = place(x, y, (1 - zh) * 4 + zl1 * 2 + far_zl0, jnp.where(master, c, 1 - c))
    dev_sib = place(x, y, z, 1 - c)
    dev_next = (lax.rem(tok + 1, 16), ch)
    dev_prev = (lax.rem(tok + 15, 16), ch)
    dev_other = (jnp.where(c == 1, lax.rem(tok + 1, 16), lax.rem(tok + 15, 16)), ch)

    barrier = pltpu.get_barrier_semaphore()
    partners = (dev_xp, dev_xm, dev_yp, dev_ym, dev_z1, dev_z2, dev_far, dev_sib, dev_other)
    for d in partners:
        pl.semaphore_signal(barrier, inc=1, device_id=d, device_id_type=MESH)
    pl.semaphore_wait(barrier, len(partners))

    w_hbm = (wv_hbm, wo_hbm)
    wbuf = (wbuf_v, wbuf_o)
    tbuf = (tbuf_v, tbuf_o)
    own, away = zl0, 1 - zl0
    names = Names()

    def slot(b, zz, j):
        return b * 8 + zz * 4 + j

    root_z = jnp.where(master, zh, 1 - zh)
    root_b = (jnp.where(master, own, away), jnp.where(master, away, own))

    def copy(name, src, dst, dev):
        i = names(name)
        return pltpu.make_async_remote_copy(
            src_ref=src, dst_ref=dst, send_sem=send_sem.at[i], recv_sem=recv_sem.at[i],
            device_id=dev, device_id_type=MESH,
        )

    def w_in(m, recv=False):
        dst = jnp.where(master, slot(away, zh, x), RELAY) if recv else jnp.where(master, RELAY, slot(own, zh, x))
        return copy(("in", m), w_hbm[m], wbuf[m].at[dst], dev_z1)

    def w_far(m, i, recv=False):
        src = w_hbm[m] if i == 0 else wbuf[m].at[RELAY]
        if recv:
            dst = slot(away if i == 0 else own, 1 - zh, x)
        else:
            dst = slot(own if i == 0 else away, zh, x)
        return copy(("far", m, i), src, wbuf[m].at[dst], dev_far)

    def w_x(m, r, way, recv=False, native=False):
        from_x = (xm if way > 0 else xp) if recv else x
        s = slot(root_b[r], root_z, from_x)
        src = w_hbm[m] if native else wbuf[m].at[s]
        return copy(("x", m, r, way), src, wbuf[m].at[s], dev_xp if way > 0 else dev_xm)

    def w_fwd(m, r, way, recv=False):
        from_x = x2 if recv else (xm if way > 0 else xp)
        rows = pl.ds(0, 256) if way > 0 else pl.ds(256, 256)
        s = wbuf[m].at[slot(root_b[r], root_z, from_x), rows]
        return copy(("fwd", m, r, way), s, s, dev_xp if way > 0 else dev_xm)

    def w_sib(m, r, k, recv=False, native=False):
        j = (x, xm, xp, x2)[k]
        s = slot(1 - root_b[r], 1 - root_z, j) if recv else slot(root_b[r], root_z, j)
        src = w_hbm[m] if native else wbuf[m].at[s]
        return copy(("sib", m, r, k), src, wbuf[m].at[s], dev_sib)

    def t_y(q, ch_, p, way, recv=False):
        first, n = (WHOLE, PARTS)[q][ch_]
        from_y = (ym if way > 0 else yp) if recv else y
        k = (zl1 if p == 0 else 1 - zl1) * 4 + from_y
        ref = tbuf[q].at[k, pl.ds(first, n)]
        src = tok_hbm if q == 0 and p == 0 else ref
        return copy(("ty", q, ch_, p, way), src, ref, dev_yp if way > 0 else dev_ym)

    def t_fwd(q, ch_, p, way, recv=False):
        first, n = (WHOLE, PARTS)[q][ch_]
        from_y = y2 if recv else (ym if way > 0 else yp)
        k = (zl1 if p == 0 else 1 - zl1) * 4 + from_y
        rows = pl.ds(first, n // 2) if way > 0 else pl.ds(first + n // 2, n // 2)
        ref = tbuf[q].at[k, rows]
        return copy(("tfwd", q, ch_, p, way), ref, ref, dev_yp if way > 0 else dev_ym)

    def t_far(q, ch_, recv=False):
        first, n = (WHOLE, PARTS)[q][ch_]
        ref = tbuf[q].at[((1 - zl1) if recv else zl1) * 4 + y, pl.ds(first, n)]
        return copy(("tz", q, ch_), tok_hbm if q == 0 else ref, ref, dev_z2)

    def partial(q, ch_):
        first, n = (WHOLE, PARTS)[q][ch_]
        rows = pl.ds(first, n)
        return copy(("c", q, ch_), part_out.at[q, rows], part_in.at[q, rows], dev_z1)

    def halo():
        return copy(("halo",), ext.at[pl.ds(ROWS, TAPS)], ext.at[pl.ds(0, TAPS)], dev_next)

    def both(make, *a):
        for way in (1, -1):
            make(*a, way).start()

    def relay_x(m, r):
        for way in (1, -1):
            w_x(m, r, way, recv=True).wait_recv()
            w_fwd(m, r, way).start()
        w_sib(m, r, 1).start()
        w_sib(m, r, 2).start()

    def end_x(m, r):
        for way in (1, -1):
            w_fwd(m, r, way, recv=True).wait_recv()
        w_sib(m, r, 3).start()

    def spread(m, r):
        both(w_x, m, r)
        w_sib(m, r, 0).start()

    def relay_y(q, ch_, p):
        for way in (1, -1):
            t_y(q, ch_, p, way, recv=True).wait_recv()
            t_fwd(q, ch_, p, way).start()

    def end_y(q, ch_, p):
        for way in (1, -1):
            t_fwd(q, ch_, p, way, recv=True).wait_recv()

    def first_w(m):
        w_in(m).start()

        @pl.when(nm)
        def _():
            w_far(m, 0).start()

    def native_w(m):
        @pl.when(master)
        def _():
            for way in (1, -1):
                w_x(m, 0, way, native=True).start()
            w_sib(m, 0, 0, native=True).start()

    def inbox_w(m):
        w_in(m, recv=True).wait_recv()

        @pl.when(master)
        def _():
            spread(m, 1)

        @pl.when(nm)
        def _():
            w_far(m, 1).start()

    def root_from_far(m, r):
        @pl.when(nm)
        def _():
            w_far(m, r, recv=True).wait_recv()
            spread(m, r)

    def local(i, src, dst):
        return pltpu.make_async_copy(src, dst, local_sem.at[i])

    def own_w(m):
        return local(m, w_hbm[m], wbuf[m].at[slot(own, zh, x)])

    t_far(0, 0).start()
    first_w(0)
    for way in (1, -1):
        t_y(0, 0, 0, way).start()
    native_w(0)
    own_tok = local(2, tok_hbm, tbuf[0].at[zl1 * 4 + y])
    own_key = local(3, key_hbm, key)
    own_query = local(4, query_hbm, query)
    own_tok.start()
    own_key.start()
    own_query.start()

    @pl.when(master)
    def _():
        own_w(0).start()
        own_w(1).start()

    s_at = lax.broadcasted_iota(jnp.int32, (TAPS, 2 * TAPS), 1)
    j_at = lax.broadcasted_iota(jnp.int32, (TAPS, 2 * TAPS), 0)
    flip = jnp.where(s_at + j_at == TAPS, 1.0, 0.0).astype(jnp.bfloat16)
    base[...] = jnp.dot(filt_ref[...].astype(jnp.bfloat16), flip, preferred_element_type=jnp.float32)

    @pl.loop(0, WIDTH // GROUP)
    def _(g):
        rows = jnp.broadcast_to(base[pl.ds(g, 1), :], (TAPS, 2 * TAPS))
        turned = pltpu.roll(rows, 0, 1, stride=1, stride_axis=0)
        band[pl.ds(pl.multiple_of(g * TAPS, TAPS), TAPS), :] = turned.astype(jnp.bfloat16)

    acc_away[...] = jnp.zeros_like(acc_away)
    acc_own[...] = jnp.zeros_like(acc_own)

    def multiply(q, acc, rows, b, zz):
        @pl.loop(0, 4)
        def _(j):
            lhs = tbuf[q][zz * 4 + j, rows, :]
            w = wbuf[q].at[slot(b, zz, j)]
            for n in range(2):
                cols = pl.ds(n * 256, 256)
                acc[rows, cols] += jnp.dot(lhs, w[:, cols], preferred_element_type=jnp.float32)

    def wait_sib(m, r):
        for k in range(4):
            w_sib(m, r, k, recv=True).wait_recv()

    inbox_w(0)
    relay_y(0, 0, 0)

    @pl.when(master)
    def _():
        relay_x(0, 0)

    root_from_far(0, 0)
    t_far(0, 0, recv=True).wait_recv()
    both(t_y, 0, 0, 1)

    @pl.when(master)
    def _():
        end_x(0, 0)
        relay_x(0, 1)

    @pl.when(nm)
    def _():
        relay_x(0, 0)

    root_from_far(0, 1)
    first_w(1)
    native_w(1)
    relay_y(0, 0, 1)
    end_y(0, 0, 0)

    @pl.when(master)
    def _():
        end_x(0, 1)

    @pl.when(nm)
    def _():
        end_x(0, 0)
        relay_x(0, 1)

    own_tok.wait()
    end_y(0, 0, 1)

    every = pl.ds(0, ROWS)

    @pl.when(master)
    def _():
        own_w(0).wait()
        own_w(1).wait()
        wait_sib(0, 0)

    @pl.when(nm)
    def _():
        wait_sib(0, 1)

    for zz in range(2):
        multiply(0, acc_away, every, away, zz)
    part_out[0] = acc_away[...].astype(jnp.bfloat16)
    partial(0, 0).start()
    inbox_w(1)

    @pl.when(master)
    def _():
        relay_x(1, 0)
        wait_sib(0, 1)

    @pl.when(nm)
    def _():
        end_x(0, 1)
        wait_sib(0, 0)

    for zz in range(2):
        multiply(0, acc_own, every, own, zz)

    root_from_far(1, 0)

    own_key.wait()
    own_query.wait()
    partial(0, 0).wait_recv()
    values = (acc_own[...] + part_in[0].astype(jnp.float32)).astype(jnp.bfloat16)
    ext[pl.ds(TAPS, ROWS), :] = (values.astype(jnp.float32) * key[...].astype(jnp.float32)).astype(jnp.bfloat16)
    halo().start()
    acc_away[...] = jnp.zeros_like(acc_away)
    acc_own[...] = jnp.zeros_like(acc_own)

    lane_group = lax.broadcasted_iota(jnp.int32, (TAPS, TAPS), 1) // GROUP
    k_own = zl1 * 4 + y

    def convolve(block):
        first = block * TAPS
        for tile in range(WIDTH // TAPS):
            lanes = pl.ds(tile * TAPS, TAPS)
            raw = jnp.dot(
                band[pl.ds(tile * 8 * TAPS, 8 * TAPS), :],
                ext[pl.ds(first, 2 * TAPS), lanes],
                preferred_element_type=jnp.float32,
            )
            conv = raw[:TAPS]
            for g in range(1, 8):
                conv = jnp.where(lane_group == g, raw[g * TAPS : (g + 1) * TAPS], conv)
            rows = pl.ds(first, TAPS)
            shaped = conv * query[rows, lanes].astype(jnp.float32)
            tbuf_o[k_own, rows, lanes] = shaped.astype(jnp.bfloat16)

    def send_shaped(ch_):
        t_far(1, ch_).start()
        both(t_y, 1, ch_, 0)

    convolve(1)
    convolve(2)
    send_shaped(0)
    root_from_far(1, 1)
    halo().wait_recv()

    @pl.when(tok == 0)
    def _():
        ext[pl.ds(0, TAPS), :] = jnp.zeros((TAPS, WIDTH), jnp.bfloat16)

    convolve(0)
    send_shaped(1)

    @pl.when(master)
    def _():
        end_x(1, 0)
        relay_x(1, 1)

    relay_y(1, 0, 0)
    t_far(1, 0, recv=True).wait_recv()
    both(t_y, 1, 0, 1)

    @pl.when(nm)
    def _():
        relay_x(1, 0)

    relay_y(1, 1, 0)
    t_far(1, 1, recv=True).wait_recv()
    both(t_y, 1, 1, 1)

    @pl.when(master)
    def _():
        end_x(1, 1)

    @pl.when(nm)
    def _():
        relay_x(1, 1)
        end_x(1, 0)

    relay_y(1, 0, 1)
    end_y(1, 0, 0)

    @pl.when(nm)
    def _():
        end_x(1, 1)

    relay_y(1, 1, 1)
    end_y(1, 0, 1)
    wait_sib(1, 0)
    wait_sib(1, 1)

    for ch_ in range(2):
        rows = pl.ds(*PARTS[ch_])
        if ch_ == 1:
            end_y(1, 1, 0)
            end_y(1, 1, 1)
        for zz in range(2):
            multiply(1, acc_away, rows, away, zz)
        part_out[1, rows] = acc_away[rows].astype(jnp.bfloat16)
        partial(1, ch_).start()
        for zz in range(2):
            multiply(1, acc_own, rows, own, zz)
    for ch_ in range(2):
        rows = pl.ds(*PARTS[ch_])
        partial(1, ch_).wait_recv()
        out_ref[rows] = (acc_own[rows] + part_in[1, rows].astype(jnp.float32)).astype(jnp.bfloat16)

    for m in range(2):
        w_in(m).wait_send()
        for r in range(2):
            for way in (1, -1):
                w_x(m, r, way).wait_send()
                w_fwd(m, r, way).wait_send()
            for k in range(4):
                w_sib(m, r, k).wait_send()

        @pl.when(nm)
        def _():
            w_far(m, 0).wait_send()
            w_far(m, 1).wait_send()

    for q, parts in ((0, WHOLE), (1, PARTS)):
        for ch_ in range(len(parts)):
            for p in range(2):
                for way in (1, -1):
                    t_y(q, ch_, p, way).wait_send()
                    t_fwd(q, ch_, p, way).wait_send()
            t_far(q, ch_).wait_send()
            partial(q, ch_).wait_send()
    halo().wait_send()


COPIES = 96


def on_device(tokens, value_weight, key_gate, query_gate, conv_filter, out_weight):
    hbm = pl.BlockSpec(memory_space=pl.ANY)
    vmem = pl.BlockSpec(memory_space=pltpu.VMEM)
    bf16, f32 = jnp.bfloat16, jnp.float32
    return pl.pallas_call(
        kernel,
        out_shape=jax.ShapeDtypeStruct((ROWS, WIDTH), bf16),
        in_specs=[hbm, hbm, hbm, hbm, vmem, hbm],
        out_specs=vmem,
        scratch_shapes=[
            pltpu.VMEM((17, WIDTH, WIDTH), bf16),
            pltpu.VMEM((17, WIDTH, WIDTH), bf16),
            pltpu.VMEM((8, ROWS, WIDTH), bf16),
            pltpu.VMEM((8, ROWS, WIDTH), bf16),
            pltpu.VMEM((WIDTH // GROUP * TAPS, 2 * TAPS), bf16),
            pltpu.VMEM((WIDTH // GROUP, 2 * TAPS), f32),
            pltpu.VMEM((TAPS + ROWS, WIDTH), bf16),
            pltpu.VMEM((ROWS, WIDTH), bf16),
            pltpu.VMEM((ROWS, WIDTH), bf16),
            pltpu.VMEM((ROWS, WIDTH), f32),
            pltpu.VMEM((ROWS, WIDTH), f32),
            pltpu.VMEM((2, ROWS, WIDTH), bf16),
            pltpu.VMEM((2, ROWS, WIDTH), bf16),
            pltpu.SemaphoreType.DMA((COPIES,)),
            pltpu.SemaphoreType.DMA((COPIES,)),
            pltpu.SemaphoreType.DMA((5,)),
        ],
        compiler_params=pltpu.CompilerParams(
            collective_id=0, has_side_effects=True, vmem_limit_bytes=56 * 1024 * 1024
        ),
        cost_estimate=pl.CostEstimate(flops=6_442_450_944, bytes_accessed=3_000_000, transcendentals=0),
        name="hyena_block",
    )(tokens, value_weight, key_gate, query_gate, conv_filter, out_weight)


def solution(mesh):
    return jax.shard_map(
        on_device,
        mesh=mesh,
        in_specs=(
            P("tok", "ch"),
            P("tok", "ch"),
            P("tok", "ch"),
            P("tok", "ch"),
            P("ch", None),
            P("tok", "ch"),
        ),
        out_specs=P("tok", "ch"),
        check_vma=False,
    )
```

```python
import functools

import jax
import jax.numpy as jnp
from jax import lax
from jax.experimental import pallas as pl
from jax.experimental.pallas import tpu as pltpu
from jax.sharding import PartitionSpec as P

MESH = pl.DeviceIdType.MESH
TAPS = 128
GROUP = 16
ROWS = 384
WIDTH = 512
HALF = WIDTH // 2
CHUNKS = (((0, 192), (192, 192)), ((128, 256), (0, 128)))
WHOLE = (0, ROWS)


class Names:
    def __init__(self):
        self.index = {}

    def __call__(self, name):
        return self.index.setdefault(name, len(self.index))


def place(x, y, z, c):
    return (x * 4 + (z // 4) * 2 + c, y * 4 + lax.rem(z, 4))


def kernel(
    tok_hbm, wv_hbm, key_hbm, query_hbm, filt_ref, wo_hbm,
    out_ref,
    wbuf_v, wbuf_o, tbuf_v, tbuf_o, band, base, ext, key, query,
    acc_away, acc_own, part_out, part_in, send_sem, recv_sem, local_sem,
):
    tok = lax.axis_index("tok")
    ch = lax.axis_index("ch")
    x, zh, c = tok // 4, lax.rem(tok // 2, 2), lax.rem(tok, 2)
    y, zl = ch // 4, lax.rem(ch, 4)
    zl1, zl0 = zl // 2, lax.rem(zl, 2)
    z = zh * 4 + zl
    master = c == zl0
    nm = jnp.logical_not(master)

    def near(zl0_):
        return zh * 4 + zl1 * 2 + zl0_

    xp, xm, x2 = lax.rem(x + 1, 4), lax.rem(x + 3, 4), lax.rem(x + 2, 4)
    yp, ym, y2 = lax.rem(y + 1, 4), lax.rem(y + 3, 4), lax.rem(y + 2, 4)
    dev_xp, dev_xm = place(xp, y, z, c), place(xm, y, z, c)
    dev_yp, dev_ym = place(x, yp, z, c), place(x, ym, z, c)
    dev_z1 = place(x, y, near(1 - zl0), c)
    dev_z2 = place(x, y, zh * 4 + (1 - zl1) * 2 + zl0, c)
    far_zl0 = jnp.where(master, zl0, 1 - zl0)
    dev_far = place(x, y, (1 - zh) * 4 + zl1 * 2 + far_zl0, jnp.where(master, c, 1 - c))
    dev_anti = place(x, y, (1 - zh) * 4 + zl, 1 - c)
    dev_sib = place(x, y, z, 1 - c)
    dev_next = (lax.rem(tok + 1, 16), ch)
    dev_prev = (lax.rem(tok + 15, 16), ch)
    dev_other = (jnp.where(c == 1, lax.rem(tok + 1, 16), lax.rem(tok + 15, 16)), ch)

    barrier = pltpu.get_barrier_semaphore()
    partners = (dev_xp, dev_xm, dev_yp, dev_ym, dev_z1, dev_z2, dev_far, dev_anti, dev_sib, dev_other)
    for d in partners:
        pl.semaphore_signal(barrier, inc=1, device_id=d, device_id_type=MESH)
    pl.semaphore_wait(barrier, len(partners))

    w_hbm = (wv_hbm, wo_hbm)
    wbuf = (wbuf_v, wbuf_o)
    tbuf = (tbuf_v, tbuf_o)
    own, away = zl0, 1 - zl0
    names = Names()

    def slot(b, zz, j):
        return b * 8 + zz * 4 + j

    root_z = jnp.where(master, zh, 1 - zh)
    root_b = (jnp.where(master, own, away), jnp.where(master, away, own))

    sent = {}
    role = ["all"]

    class Sent:
        def __init__(self, name, src, dst, dev):
            i = names(name)
            self.name = name
            self.make = lambda: pltpu.make_async_remote_copy(
                src_ref=src, dst_ref=dst, send_sem=send_sem.at[i], recv_sem=recv_sem.at[i],
                device_id=dev, device_id_type=MESH,
            )

        def start(self):
            sent.setdefault(self.name, set()).add(role[0])
            self.make().start()

        def wait_recv(self):
            self.make().wait_recv()

        def wait_send(self):
            self.make().wait_send()

    copy = Sent

    def when_master(body):
        role[0] = "master"
        pl.when(master)(body)
        role[0] = "all"

    def when_not(body):
        role[0] = "nm"
        pl.when(nm)(body)
        role[0] = "all"

    def half(h):
        return pl.ds(h * HALF, HALF)

    def w_in(m, h, recv=False):
        s = slot(away if recv else own, zh, x)
        return copy(("in", m, h), w_hbm[m].at[half(h)], wbuf[m].at[s, half(h)], dev_z1)

    def w_far(m, h, recv=False):
        s = slot(away, 1 - zh, x) if recv else slot(own, zh, x)
        return copy(("far", m, h), w_hbm[m].at[half(h)], wbuf[m].at[s, half(h)], dev_far)

    def w_anti(m, h, recv=False):
        s = slot(own, 1 - zh, x) if recv else slot(own, zh, x)
        return copy(("anti", m, h), w_hbm[m].at[half(h)], wbuf[m].at[s, half(h)], dev_anti)

    def w_x(m, r, way, h, recv=False, native=False):
        from_x = (xm if way > 0 else xp) if recv else x
        dst = wbuf[m].at[slot(root_b[r], root_z, from_x), half(h)]
        src = w_hbm[m].at[half(h)] if native else dst
        return copy(("x", m, r, way, h), src, dst, dev_xp if way > 0 else dev_xm)

    def w_fwd(m, r, way, recv=False):
        from_x = x2 if recv else (xm if way > 0 else xp)
        s = wbuf[m].at[slot(root_b[r], root_z, from_x), half(first_half(way))]
        return copy(("fwd", m, r, way), s, s, dev_xp if way > 0 else dev_xm)

    def w_sib(m, r, k, recv=False, native=False):
        j = (x, xm, xp, x2)[k]
        s = slot(1 - root_b[r], 1 - root_z, j) if recv else slot(root_b[r], root_z, j)
        src = w_hbm[m] if native else wbuf[m].at[s]
        return copy(("sib", m, r, k), src, wbuf[m].at[s], dev_sib)

    def first_half(way):
        return 0 if way > 0 else 1

    def t_y(q, ch_, p, way, h, recv=False):
        first, n = CHUNKS[q][ch_]
        from_y = (ym if way > 0 else yp) if recv else y
        k = (zl1 if p == 0 else 1 - zl1) * 4 + from_y
        rows = pl.ds(first + h * (n // 2), n // 2)
        ref = tbuf[q].at[k, rows]
        src = tok_hbm.at[rows] if q == 0 and p == 0 else ref
        return copy(("ty", q, ch_, p, way, h), src, ref, dev_yp if way > 0 else dev_ym)

    def t_fwd(q, ch_, p, way, recv=False):
        first, n = CHUNKS[q][ch_]
        from_y = y2 if recv else (ym if way > 0 else yp)
        k = (zl1 if p == 0 else 1 - zl1) * 4 + from_y
        ref = tbuf[q].at[k, pl.ds(first + first_half(way) * (n // 2), n // 2)]
        return copy(("tfwd", q, ch_, p, way), ref, ref, dev_yp if way > 0 else dev_ym)

    def t_far(q, ch_, recv=False):
        first, n = CHUNKS[q][ch_]
        ref = tbuf[q].at[((1 - zl1) if recv else zl1) * 4 + y, pl.ds(first, n)]
        src = tok_hbm.at[pl.ds(first, n)] if q == 0 else ref
        return copy(("tz", q, ch_), src, ref, dev_z2)

    def partial(q, ch_):
        rows = pl.ds(*(WHOLE if q == 0 else CHUNKS[1][ch_]))
        return copy(("c", q, ch_), part_out.at[q, rows], part_in.at[q, rows], dev_z1)

    def halo():
        return copy(("halo",), ext.at[pl.ds(ROWS, TAPS)], ext.at[pl.ds(0, TAPS)], dev_next)

    senders = {
        "in": w_in, "far": w_far, "anti": w_anti, "x": w_x, "fwd": w_fwd, "sib": w_sib,
        "ty": t_y, "tfwd": t_fwd, "tz": t_far, "c": partial, "halo": halo,
    }

    def send_x(m, r, native=False):
        for h in range(2):
            for way in (1, -1):
                w_x(m, r, way, h if way > 0 else 1 - h, native=native).start()

    def relay_x(m, r):
        for way in (1, -1):
            w_x(m, r, way, first_half(way), recv=True).wait_recv()
            w_fwd(m, r, way).start()

    def mid_x(m, r):
        for way in (1, -1):
            w_x(m, r, way, 1 - first_half(way), recv=True).wait_recv()
        w_sib(m, r, 1).start()
        w_sib(m, r, 2).start()

    def end_x(m, r):
        for way in (1, -1):
            w_fwd(m, r, way, recv=True).wait_recv()
        w_sib(m, r, 3).start()

    def take_root(m, r, arrival):
        for h in range(2):
            arrival(m, h, recv=True).wait_recv()
            for way in (1, -1):
                w_x(m, r, way, h).start()
        w_sib(m, r, 0).start()

    def send_y(q, ch_, p):
        for h in range(2):
            for way in (1, -1):
                t_y(q, ch_, p, way, h if way > 0 else 1 - h).start()

    def relay_y(q, ch_, p):
        for way in (1, -1):
            t_y(q, ch_, p, way, first_half(way), recv=True).wait_recv()
            t_fwd(q, ch_, p, way).start()

    def end_y(q, ch_, p):
        for way in (1, -1):
            t_y(q, ch_, p, way, 1 - first_half(way), recv=True).wait_recv()
            t_fwd(q, ch_, p, way, recv=True).wait_recv()

    def far_y(q, ch_):
        t_far(q, ch_, recv=True).wait_recv()
        send_y(q, ch_, 1)

    def z_not(m):
        for send in (w_in, w_far):
            for h in range(2):
                send(m, h).start()

    def z_master(m):
        for h in range(2):
            w_anti(m, h).start()

    def x_master(m):
        send_x(m, 0, native=True)
        w_sib(m, 0, 0, native=True).start()

    def local(i, src, dst):
        return pltpu.make_async_copy(src, dst, local_sem.at[i])

    def own_w(m):
        return local(m, w_hbm[m], wbuf[m].at[slot(own, zh, x)])

    for ch_ in range(2):
        t_far(0, ch_).start()

    @when_not
    def _():
        z_not(0)

    @when_master
    def _():
        x_master(0)

    for ch_ in range(2):
        send_y(0, ch_, 0)

    @when_master
    def _():
        z_master(0)

    own_tok = local(2, tok_hbm, tbuf[0].at[zl1 * 4 + y])
    own_key = local(3, key_hbm, key)
    own_query = local(4, query_hbm, query)
    own_tok.start()
    own_key.start()
    own_query.start()

    @when_master
    def _():
        own_w(0).start()
        own_w(1).start()

    s_at = lax.broadcasted_iota(jnp.int32, (TAPS, 2 * TAPS), 1)
    j_at = lax.broadcasted_iota(jnp.int32, (TAPS, 2 * TAPS), 0)
    flip = jnp.where(s_at + j_at == TAPS, 1.0, 0.0).astype(jnp.bfloat16)
    base[...] = jnp.dot(filt_ref[...].astype(jnp.bfloat16), flip, preferred_element_type=jnp.float32)

    @pl.loop(0, WIDTH // GROUP)
    def _(g):
        rows = jnp.broadcast_to(base[pl.ds(g, 1), :], (TAPS, 2 * TAPS))
        turned = pltpu.roll(rows, 0, 1, stride=1, stride_axis=0)
        band[pl.ds(pl.multiple_of(g * TAPS, TAPS), TAPS), :] = turned.astype(jnp.bfloat16)

    acc_away[...] = jnp.zeros_like(acc_away)
    acc_own[...] = jnp.zeros_like(acc_own)

    def multiply(q, acc, rows, b, zz):
        @pl.loop(0, 4)
        def _(j):
            lhs = tbuf[q][zz * 4 + j, rows, :]
            w = wbuf[q].at[slot(b, zz, j)]
            for n in range(2):
                cols = pl.ds(n * 256, 256)
                acc[rows, cols] += jnp.dot(lhs, w[:, cols], preferred_element_type=jnp.float32)

    def wait_sib(m, r):
        for k in range(4):
            w_sib(m, r, k, recv=True).wait_recv()

    relay_y(0, 0, 0)
    relay_y(0, 1, 0)

    @when_master
    def _():
        relay_x(0, 0)
        take_root(0, 1, w_in)
        mid_x(0, 0)

    far_y(0, 0)

    @when_not
    def _():
        take_root(0, 0, w_far)

    far_y(0, 1)

    @when_master
    def _():
        end_x(0, 0)
        relay_x(0, 1)
        x_master(1)

    @when_not
    def _():
        relay_x(0, 0)

    relay_y(0, 0, 1)

    @when_not
    def _():
        take_root(0, 1, w_anti)
        z_not(1)

    relay_y(0, 1, 1)

    @when_master
    def _():
        mid_x(0, 1)
        end_x(0, 1)
        z_master(1)

    @when_not
    def _():
        mid_x(0, 0)
        end_x(0, 0)
        relay_x(0, 1)

    own_tok.wait()
    for p in range(2):
        for ch_ in range(2):
            end_y(0, ch_, p)

    every = pl.ds(0, ROWS)

    @when_master
    def _():
        own_w(0).wait()
        own_w(1).wait()
        wait_sib(0, 0)

    @when_not
    def _():
        wait_sib(0, 1)

    for zz in range(2):
        multiply(0, acc_away, every, away, zz)
    part_out[0] = acc_away[...].astype(jnp.bfloat16)
    partial(0, 0).start()

    @when_master
    def _():
        relay_x(1, 0)
        take_root(1, 1, w_in)
        wait_sib(0, 1)

    @when_not
    def _():
        mid_x(0, 1)
        end_x(0, 1)
        wait_sib(0, 0)

    for zz in range(2):
        multiply(0, acc_own, every, own, zz)

    @when_not
    def _():
        take_root(1, 0, w_far)

    own_key.wait()
    own_query.wait()
    partial(0, 0).wait_recv()
    values = (acc_own[...] + part_in[0].astype(jnp.float32)).astype(jnp.bfloat16)
    ext[pl.ds(TAPS, ROWS), :] = (values.astype(jnp.float32) * key[...].astype(jnp.float32)).astype(jnp.bfloat16)
    halo().start()
    acc_away[...] = jnp.zeros_like(acc_away)
    acc_own[...] = jnp.zeros_like(acc_own)

    lane_group = lax.broadcasted_iota(jnp.int32, (TAPS, TAPS), 1) // GROUP
    k_own = zl1 * 4 + y

    def convolve(block):
        first = block * TAPS
        for tile in range(WIDTH // TAPS):
            lanes = pl.ds(tile * TAPS, TAPS)
            raw = jnp.dot(
                band[pl.ds(tile * 8 * TAPS, 8 * TAPS), :],
                ext[pl.ds(first, 2 * TAPS), lanes],
                preferred_element_type=jnp.float32,
            )
            conv = raw[:TAPS]
            for g in range(1, 8):
                conv = jnp.where(lane_group == g, raw[g * TAPS : (g + 1) * TAPS], conv)
            rows = pl.ds(first, TAPS)
            shaped = conv * query[rows, lanes].astype(jnp.float32)
            tbuf_o[k_own, rows, lanes] = shaped.astype(jnp.bfloat16)

    def send_shaped(ch_):
        t_far(1, ch_).start()
        send_y(1, ch_, 0)

    convolve(1)
    convolve(2)
    send_shaped(0)
    halo().wait_recv()

    @pl.when(tok == 0)
    def _():
        ext[pl.ds(0, TAPS), :] = jnp.zeros((TAPS, WIDTH), jnp.bfloat16)

    convolve(0)
    send_shaped(1)

    @when_master
    def _():
        mid_x(1, 0)
        end_x(1, 0)
        relay_x(1, 1)

    @when_not
    def _():
        relay_x(1, 0)

    relay_y(1, 0, 0)
    far_y(1, 0)

    @when_not
    def _():
        take_root(1, 1, w_anti)

    relay_y(1, 1, 0)
    far_y(1, 1)

    @when_master
    def _():
        mid_x(1, 1)
        end_x(1, 1)

    @when_not
    def _():
        mid_x(1, 0)
        end_x(1, 0)
        relay_x(1, 1)

    relay_y(1, 0, 1)
    end_y(1, 0, 0)
    relay_y(1, 1, 1)

    @when_not
    def _():
        mid_x(1, 1)
        end_x(1, 1)

    end_y(1, 0, 1)
    wait_sib(1, 0)
    wait_sib(1, 1)

    for ch_ in range(2):
        rows = pl.ds(*CHUNKS[1][ch_])
        if ch_ == 1:
            end_y(1, 1, 0)
            end_y(1, 1, 1)
        for zz in range(2):
            multiply(1, acc_away, rows, away, zz)
        part_out[1, rows] = acc_away[rows].astype(jnp.bfloat16)
        partial(1, ch_).start()
        for zz in range(2):
            multiply(1, acc_own, rows, own, zz)
    for ch_ in range(2):
        rows = pl.ds(*CHUNKS[1][ch_])
        partial(1, ch_).wait_recv()
        out_ref[rows] = (acc_own[rows] + part_in[1, rows].astype(jnp.float32)).astype(jnp.bfloat16)

    def last(only):
        for name, roles in sent.items():
            if ("all" in roles or len(roles) == 2) == (only == "all") and (only == "all" or only in roles):
                senders[name[0]](*name[1:]).wait_send()

    last("all")

    @when_master
    def _():
        last("master")

    @when_not
    def _():
        last("nm")


COPIES = 128


def on_device(tokens, value_weight, key_gate, query_gate, conv_filter, out_weight):
    hbm = pl.BlockSpec(memory_space=pl.ANY)
    vmem = pl.BlockSpec(memory_space=pltpu.VMEM)
    bf16, f32 = jnp.bfloat16, jnp.float32
    return pl.pallas_call(
        kernel,
        out_shape=jax.ShapeDtypeStruct((ROWS, WIDTH), bf16),
        in_specs=[hbm, hbm, hbm, hbm, vmem, hbm],
        out_specs=vmem,
        scratch_shapes=[
            pltpu.VMEM((16, WIDTH, WIDTH), bf16),
            pltpu.VMEM((16, WIDTH, WIDTH), bf16),
            pltpu.VMEM((8, ROWS, WIDTH), bf16),
            pltpu.VMEM((8, ROWS, WIDTH), bf16),
            pltpu.VMEM((WIDTH // GROUP * TAPS, 2 * TAPS), bf16),
            pltpu.VMEM((WIDTH // GROUP, 2 * TAPS), f32),
            pltpu.VMEM((TAPS + ROWS, WIDTH), bf16),
            pltpu.VMEM((ROWS, WIDTH), bf16),
            pltpu.VMEM((ROWS, WIDTH), bf16),
            pltpu.VMEM((ROWS, WIDTH), f32),
            pltpu.VMEM((ROWS, WIDTH), f32),
            pltpu.VMEM((2, ROWS, WIDTH), bf16),
            pltpu.VMEM((2, ROWS, WIDTH), bf16),
            pltpu.SemaphoreType.DMA((COPIES,)),
            pltpu.SemaphoreType.DMA((COPIES,)),
            pltpu.SemaphoreType.DMA((5,)),
        ],
        compiler_params=pltpu.CompilerParams(
            collective_id=0, has_side_effects=True, vmem_limit_bytes=56 * 1024 * 1024
        ),
        cost_estimate=pl.CostEstimate(flops=6_442_450_944, bytes_accessed=3_000_000, transcendentals=0),
        name="hyena_block",
    )(tokens, value_weight, key_gate, query_gate, conv_filter, out_weight)


def solution(mesh):
    return jax.shard_map(
        on_device,
        mesh=mesh,
        in_specs=(
            P("tok", "ch"),
            P("tok", "ch"),
            P("tok", "ch"),
            P("tok", "ch"),
            P("ch", None),
            P("tok", "ch"),
        ),
        out_specs=P("tok", "ch"),
        check_vma=False,
    )
```

```python
import functools

import jax
import jax.numpy as jnp
from jax import lax
from jax.experimental import pallas as pl
from jax.experimental.pallas import tpu as pltpu
from jax.sharding import PartitionSpec as P

MESH = pl.DeviceIdType.MESH
TAPS = 128
GROUP = 16
ROWS = 384
WIDTH = 512
HALF = WIDTH // 2
CHUNKS = (((0, 192), (192, 192)), ((128, 256), (0, 128)))
WHOLE = (0, ROWS)


class Names:
    def __init__(self):
        self.index = {}

    def __call__(self, name):
        return self.index.setdefault(name, len(self.index))


def place(x, y, z, c):
    return (x * 4 + (z // 4) * 2 + c, y * 4 + lax.rem(z, 4))


def kernel(
    tok_hbm, wv_hbm, key_hbm, query_hbm, filt_ref, wo_hbm,
    out_ref,
    wbuf_v, wbuf_o, tbuf_v, tbuf_o, band, base, ext, key, query,
    acc_away, acc_own, part_out, part_in, send_sem, recv_sem, local_sem,
):
    tok = lax.axis_index("tok")
    ch = lax.axis_index("ch")
    x, zh, c = tok // 4, lax.rem(tok // 2, 2), lax.rem(tok, 2)
    y, zl = ch // 4, lax.rem(ch, 4)
    zl1, zl0 = zl // 2, lax.rem(zl, 2)
    z = zh * 4 + zl
    master = c == zl0
    nm = jnp.logical_not(master)

    def near(zl0_):
        return zh * 4 + zl1 * 2 + zl0_

    xp, xm, x2 = lax.rem(x + 1, 4), lax.rem(x + 3, 4), lax.rem(x + 2, 4)
    yp, ym, y2 = lax.rem(y + 1, 4), lax.rem(y + 3, 4), lax.rem(y + 2, 4)
    dev_xp, dev_xm = place(xp, y, z, c), place(xm, y, z, c)
    dev_yp, dev_ym = place(x, yp, z, c), place(x, ym, z, c)
    dev_z1 = place(x, y, near(1 - zl0), c)
    dev_z2 = place(x, y, zh * 4 + (1 - zl1) * 2 + zl0, c)
    far_zl0 = jnp.where(master, zl0, 1 - zl0)
    dev_far = place(x, y, (1 - zh) * 4 + zl1 * 2 + far_zl0, jnp.where(master, c, 1 - c))
    dev_anti = place(x, y, (1 - zh) * 4 + zl, 1 - c)
    dev_sib = place(x, y, z, 1 - c)
    dev_next = (lax.rem(tok + 1, 16), ch)
    dev_prev = (lax.rem(tok + 15, 16), ch)
    dev_other = (jnp.where(c == 1, lax.rem(tok + 1, 16), lax.rem(tok + 15, 16)), ch)

    barrier = pltpu.get_barrier_semaphore()
    partners = (dev_xp, dev_xm, dev_yp, dev_ym, dev_z1, dev_z2, dev_far, dev_anti, dev_sib, dev_other)
    for d in partners:
        pl.semaphore_signal(barrier, inc=1, device_id=d, device_id_type=MESH)
    pl.semaphore_wait(barrier, len(partners))

    w_hbm = (wv_hbm, wo_hbm)
    wbuf = (wbuf_v, wbuf_o)
    tbuf = (tbuf_v, tbuf_o)
    own, away = zl0, 1 - zl0
    names = Names()

    def slot(b, zz, j):
        return b * 8 + zz * 4 + j

    root_z = jnp.where(master, zh, 1 - zh)
    root_b = (jnp.where(master, own, away), jnp.where(master, away, own))

    sent = {}
    role = ["all"]

    class Sent:
        def __init__(self, name, src, dst, dev):
            i = names(name)
            self.name = name
            self.make = lambda: pltpu.make_async_remote_copy(
                src_ref=src, dst_ref=dst, send_sem=send_sem.at[i], recv_sem=recv_sem.at[i],
                device_id=dev, device_id_type=MESH,
            )

        def start(self):
            sent.setdefault(self.name, set()).add(role[0])
            self.make().start()

        def wait_recv(self):
            self.make().wait_recv()

        def wait_send(self):
            self.make().wait_send()

    copy = Sent

    def when_master(body):
        role[0] = "master"
        pl.when(master)(body)
        role[0] = "all"

    def when_not(body):
        role[0] = "nm"
        pl.when(nm)(body)
        role[0] = "all"

    def half(h):
        return pl.ds(h * HALF, HALF)

    def w_in(m, h, recv=False):
        s = slot(away if recv else own, zh, x)
        return copy(("in", m, h), w_hbm[m].at[half(h)], wbuf[m].at[s, half(h)], dev_z1)

    def w_far(m, h, recv=False):
        s = slot(away, 1 - zh, x) if recv else slot(own, zh, x)
        return copy(("far", m, h), w_hbm[m].at[half(h)], wbuf[m].at[s, half(h)], dev_far)

    def w_anti(m, h, recv=False):
        s = slot(own, 1 - zh, x) if recv else slot(own, zh, x)
        return copy(("anti", m, h), w_hbm[m].at[half(h)], wbuf[m].at[s, half(h)], dev_anti)

    def w_x(m, r, way, h, recv=False, native=False):
        from_x = (xm if way > 0 else xp) if recv else x
        dst = wbuf[m].at[slot(root_b[r], root_z, from_x), half(h)]
        src = w_hbm[m].at[half(h)] if native else dst
        return copy(("x", m, r, way, h), src, dst, dev_xp if way > 0 else dev_xm)

    def w_fwd(m, r, way, recv=False):
        from_x = x2 if recv else (xm if way > 0 else xp)
        s = wbuf[m].at[slot(root_b[r], root_z, from_x), half(first_half(way))]
        return copy(("fwd", m, r, way), s, s, dev_xp if way > 0 else dev_xm)

    def w_sib(m, r, k, recv=False, native=False):
        j = (x, xm, xp, x2)[k]
        s = slot(1 - root_b[r], 1 - root_z, j) if recv else slot(root_b[r], root_z, j)
        src = w_hbm[m] if native else wbuf[m].at[s]
        return copy(("sib", m, r, k), src, wbuf[m].at[s], dev_sib)

    def first_half(way):
        return 0 if way > 0 else 1

    def t_y(q, ch_, p, way, h, recv=False):
        first, n = CHUNKS[q][ch_]
        from_y = (ym if way > 0 else yp) if recv else y
        k = (zl1 if p == 0 else 1 - zl1) * 4 + from_y
        rows = pl.ds(first + h * (n // 2), n // 2)
        ref = tbuf[q].at[k, rows]
        src = tok_hbm.at[rows] if q == 0 and p == 0 else ref
        return copy(("ty", q, ch_, p, way, h), src, ref, dev_yp if way > 0 else dev_ym)

    def t_fwd(q, ch_, p, way, recv=False):
        first, n = CHUNKS[q][ch_]
        from_y = y2 if recv else (ym if way > 0 else yp)
        k = (zl1 if p == 0 else 1 - zl1) * 4 + from_y
        ref = tbuf[q].at[k, pl.ds(first + first_half(way) * (n // 2), n // 2)]
        return copy(("tfwd", q, ch_, p, way), ref, ref, dev_yp if way > 0 else dev_ym)

    def t_far(q, ch_, recv=False):
        first, n = CHUNKS[q][ch_]
        ref = tbuf[q].at[((1 - zl1) if recv else zl1) * 4 + y, pl.ds(first, n)]
        src = tok_hbm.at[pl.ds(first, n)] if q == 0 else ref
        return copy(("tz", q, ch_), src, ref, dev_z2)

    def partial(q, ch_):
        rows = pl.ds(*(WHOLE if q == 0 else CHUNKS[1][ch_]))
        return copy(("c", q, ch_), part_out.at[q, rows], part_in.at[q, rows], dev_z1)

    def halo():
        return copy(("halo",), ext.at[pl.ds(ROWS, TAPS)], ext.at[pl.ds(0, TAPS)], dev_next)

    senders = {
        "in": w_in, "far": w_far, "anti": w_anti, "x": w_x, "fwd": w_fwd, "sib": w_sib,
        "ty": t_y, "tfwd": t_fwd, "tz": t_far, "c": partial, "halo": halo,
    }

    def send_x(m, r, native=False):
        for h in range(2):
            for way in (1, -1):
                w_x(m, r, way, h if way > 0 else 1 - h, native=native).start()

    def relay_x(m, r):
        for way in (1, -1):
            w_x(m, r, way, first_half(way), recv=True).wait_recv()
            w_fwd(m, r, way).start()

    def mid_x(m, r):
        for way in (1, -1):
            w_x(m, r, way, 1 - first_half(way), recv=True).wait_recv()
        w_sib(m, r, 1).start()
        w_sib(m, r, 2).start()

    def end_x(m, r):
        for way in (1, -1):
            w_fwd(m, r, way, recv=True).wait_recv()
        w_sib(m, r, 3).start()

    def take_half(m, r, h, arrival):
        arrival(m, h, recv=True).wait_recv()
        for way in (1, -1):
            w_x(m, r, way, h).start()
        if h == 1:
            w_sib(m, r, 0).start()

    def send_y(q, ch_, p):
        for h in range(2):
            for way in (1, -1):
                t_y(q, ch_, p, way, h if way > 0 else 1 - h).start()

    def relay_y(q, ch_, p):
        for way in (1, -1):
            t_y(q, ch_, p, way, first_half(way), recv=True).wait_recv()
            t_fwd(q, ch_, p, way).start()

    def end_y(q, ch_, p):
        for way in (1, -1):
            t_y(q, ch_, p, way, 1 - first_half(way), recv=True).wait_recv()
            t_fwd(q, ch_, p, way, recv=True).wait_recv()

    def far_y(q, ch_):
        t_far(q, ch_, recv=True).wait_recv()
        send_y(q, ch_, 1)

    def z_in(m, h):
        w_in(m, h).start()

    def z_far(m, h):
        w_far(m, h).start()

    def z_anti(m, h):
        w_anti(m, h).start()

    def t_z(ch_):
        t_far(0, ch_).start()

    def x_master(m):
        send_x(m, 0, native=True)
        w_sib(m, 0, 0, native=True).start()

    def local(i, src, dst):
        return pltpu.make_async_copy(src, dst, local_sem.at[i])

    def own_w(m):
        return local(m, w_hbm[m], wbuf[m].at[slot(own, zh, x)])


    @when_not
    def _():
        z_in(0, 0)


    @when_master
    def _():
        x_master(0)

    t_z(0)

    @when_not
    def _():
        z_far(0, 0)


    own_tok = local(2, tok_hbm, tbuf[0].at[zl1 * 4 + y])
    own_key = local(3, key_hbm, key)
    own_query = local(4, query_hbm, query)
    own_tok.start()
    own_key.start()
    own_query.start()

    @when_master
    def _():
        own_w(0).start()
        own_w(1).start()

    s_at = lax.broadcasted_iota(jnp.int32, (TAPS, 2 * TAPS), 1)
    j_at = lax.broadcasted_iota(jnp.int32, (TAPS, 2 * TAPS), 0)
    flip = jnp.where(s_at + j_at == TAPS, 1.0, 0.0).astype(jnp.bfloat16)
    base[...] = jnp.dot(filt_ref[...].astype(jnp.bfloat16), flip, preferred_element_type=jnp.float32)

    @pl.loop(0, WIDTH // GROUP)
    def _(g):
        rows = jnp.broadcast_to(base[pl.ds(g, 1), :], (TAPS, 2 * TAPS))
        turned = pltpu.roll(rows, 0, 1, stride=1, stride_axis=0)
        band[pl.ds(pl.multiple_of(g * TAPS, TAPS), TAPS), :] = turned.astype(jnp.bfloat16)

    acc_away[...] = jnp.zeros_like(acc_away)
    acc_own[...] = jnp.zeros_like(acc_own)

    def multiply(q, acc, rows, b, zz):
        for n in range(2):
            cols = pl.ds(n * 256, 256)
            total = None
            for j in range(4):
                term = jnp.dot(
                    tbuf[q][zz * 4 + j, rows, :],
                    wbuf[q][slot(b, zz, j), :, cols],
                    preferred_element_type=jnp.float32,
                )
                total = term if total is None else total + term
            acc[rows, cols] += total

    def wait_sib(m, r):
        for k in range(4):
            w_sib(m, r, k, recv=True).wait_recv()

    every = pl.ds(0, ROWS)
    k_own = zl1 * 4 + y

    def convolve(blocks):
        width = len(blocks) * TAPS
        lane_group = lax.rem(lax.broadcasted_iota(jnp.int32, (TAPS, width), 1), TAPS) // GROUP
        for tile in range(WIDTH // TAPS):
            lanes = pl.ds(tile * TAPS, TAPS)
            parts = [ext[pl.ds(block * TAPS, 2 * TAPS), lanes] for block in blocks]
            window = parts[0] if len(parts) == 1 else jnp.concatenate(parts, axis=1)
            conv = None
            for g in range(8):
                raw = jnp.dot(
                    band[pl.ds((tile * 8 + g) * TAPS, TAPS), :], window, preferred_element_type=jnp.float32
                )
                conv = raw if conv is None else jnp.where(lane_group == g, raw, conv)
            for i, block in enumerate(blocks):
                rows = pl.ds(block * TAPS, TAPS)
                shaped = conv[:, i * TAPS : (i + 1) * TAPS] * query[rows, lanes].astype(jnp.float32)
                tbuf_o[k_own, rows, lanes] = shaped.astype(jnp.bfloat16)

    def send_shaped(ch_):
        t_far(1, ch_).start()
        send_y(1, ch_, 0)

    def away0():
        own_tok.wait()

        @pl.when(master)
        def _():
            own_w(0).wait()
            own_w(1).wait()

        for zz in range(2):
            multiply(0, acc_away, every, away, zz)
        part_out[0] = acc_away[...].astype(jnp.bfloat16)
        partial(0, 0).start()
        acc_away[...] = jnp.zeros_like(acc_away)

    def own0():
        for zz in range(2):
            multiply(0, acc_own, every, own, zz)

    def gate():
        own_key.wait()
        own_query.wait()
        partial(0, 0).wait_recv()
        values = (acc_own[...] + part_in[0].astype(jnp.float32)).astype(jnp.bfloat16)
        ext[pl.ds(TAPS, ROWS), :] = (values.astype(jnp.float32) * key[...].astype(jnp.float32)).astype(jnp.bfloat16)
        halo().start()
        convolve((1, 2))
        send_shaped(0)
        acc_own[...] = jnp.zeros_like(acc_own)

    def rim():
        halo().wait_recv()

        @pl.when(tok == 0)
        def _():
            ext[pl.ds(0, TAPS), :] = jnp.zeros((TAPS, WIDTH), jnp.bfloat16)

        convolve((0,))
        send_shaped(1)

    def near2(ch_):
        rows = pl.ds(*CHUNKS[1][ch_])
        multiply(1, acc_away, rows, away, zl1)
        multiply(1, acc_own, rows, own, zl1)

    def far2(ch_):
        rows = pl.ds(*CHUNKS[1][ch_])
        multiply(1, acc_away, rows, away, 1 - zl1)
        part_out[1, rows] = acc_away[rows].astype(jnp.bfloat16)
        partial(1, ch_).start()
        multiply(1, acc_own, rows, own, 1 - zl1)

    def result(ch_):
        rows = pl.ds(*CHUNKS[1][ch_])
        partial(1, ch_).wait_recv()
        out_ref[rows] = (acc_own[rows] + part_in[1, rows].astype(jnp.float32)).astype(jnp.bfloat16)


    @when_master
    def _():
        x_master(1)

    send_y(0, 0, 0)

    @when_master
    def _():
        take_half(0, 1, 0, w_in)
        take_half(0, 1, 1, w_in)
        z_anti(0, 1)


    @when_not
    def _():
        z_in(0, 1)

    relay_y(0, 0, 0)
    send_y(0, 1, 0)

    @when_master
    def _():
        relay_x(0, 0)
        end_x(0, 0)
        relay_x(0, 1)


    @when_not
    def _():
        z_far(0, 1)

    relay_y(0, 1, 0)

    @when_master
    def _():
        z_anti(0, 0)


    @when_not
    def _():
        z_in(1, 1)

    far_y(0, 0)

    @when_master
    def _():
        mid_x(0, 0)


    @when_not
    def _():
        take_half(0, 0, 0, w_far)

    t_z(1)

    @when_not
    def _():
        take_half(0, 0, 1, w_far)

    far_y(0, 1)
    end_y(0, 0, 0)

    @when_master
    def _():
        mid_x(0, 1)
        z_anti(1, 0)
        end_x(0, 1)

    relay_y(0, 1, 1)
    relay_y(0, 0, 1)

    @when_master
    def _():
        take_half(1, 1, 0, w_in)
        wait_sib(0, 0)


    @when_not
    def _():
        relay_x(0, 0)
        z_far(1, 0)
        take_half(0, 1, 0, w_anti)
        z_in(1, 0)
        z_far(1, 1)
        take_half(0, 1, 1, w_anti)

    end_y(0, 1, 1)

    @when_not
    def _():
        mid_x(0, 0)
        end_x(0, 0)

    end_y(0, 0, 1)

    @when_not
    def _():
        relay_x(0, 1)

    end_y(0, 1, 0)

    @when_not
    def _():
        mid_x(0, 1)
        wait_sib(0, 1)
        wait_sib(0, 0)

    away0()

    @when_master
    def _():
        wait_sib(0, 1)
        take_half(1, 1, 1, w_in)


    @when_not
    def _():
        take_half(1, 0, 0, w_far)
        end_x(0, 1)
        take_half(1, 1, 0, w_anti)

    own0()

    @when_master
    def _():
        z_anti(1, 1)
        relay_x(1, 1)
        relay_x(1, 0)


    @when_not
    def _():
        take_half(1, 0, 1, w_far)

    gate()

    @when_master
    def _():
        mid_x(1, 0)

    relay_y(1, 0, 0)

    @when_master
    def _():
        end_x(1, 0)


    @when_not
    def _():
        relay_x(1, 0)

    rim()

    @when_master
    def _():
        mid_x(1, 1)

    far_y(1, 0)
    relay_y(1, 1, 0)

    @when_master
    def _():
        end_x(1, 1)


    @when_not
    def _():
        take_half(1, 1, 1, w_anti)

    far_y(1, 1)

    @when_not
    def _():
        relay_x(1, 1)

    relay_y(1, 0, 1)

    @when_not
    def _():
        end_x(1, 0)

    end_y(1, 0, 0)

    @when_not
    def _():
        mid_x(1, 0)

    wait_sib(1, 1)

    @when_not
    def _():
        mid_x(1, 1)
        end_x(1, 1)

    wait_sib(1, 0)
    end_y(1, 1, 0)
    near2(1)
    near2(0)
    relay_y(1, 1, 1)
    end_y(1, 0, 1)
    far2(0)
    end_y(1, 1, 1)
    far2(1)
    result(1)
    result(0)

    def last(only):
        for name, roles in sent.items():
            if ("all" in roles or len(roles) == 2) == (only == "all") and (only == "all" or only in roles):
                senders[name[0]](*name[1:]).wait_send()

    last("all")

    @when_master
    def _():
        last("master")

    @when_not
    def _():
        last("nm")


COPIES = 128


def on_device(tokens, value_weight, key_gate, query_gate, conv_filter, out_weight):
    hbm = pl.BlockSpec(memory_space=pl.ANY)
    vmem = pl.BlockSpec(memory_space=pltpu.VMEM)
    bf16, f32 = jnp.bfloat16, jnp.float32
    return pl.pallas_call(
        kernel,
        out_shape=jax.ShapeDtypeStruct((ROWS, WIDTH), bf16),
        in_specs=[hbm, hbm, hbm, hbm, vmem, hbm],
        out_specs=vmem,
        scratch_shapes=[
            pltpu.VMEM((16, WIDTH, WIDTH), bf16),
            pltpu.VMEM((16, WIDTH, WIDTH), bf16),
            pltpu.VMEM((8, ROWS, WIDTH), bf16),
            pltpu.VMEM((8, ROWS, WIDTH), bf16),
            pltpu.VMEM((WIDTH // GROUP * TAPS, 2 * TAPS), bf16),
            pltpu.VMEM((WIDTH // GROUP, 2 * TAPS), f32),
            pltpu.VMEM((TAPS + ROWS, WIDTH), bf16),
            pltpu.VMEM((ROWS, WIDTH), bf16),
            pltpu.VMEM((ROWS, WIDTH), bf16),
            pltpu.VMEM((ROWS, WIDTH), f32),
            pltpu.VMEM((ROWS, WIDTH), f32),
            pltpu.VMEM((2, ROWS, WIDTH), bf16),
            pltpu.VMEM((2, ROWS, WIDTH), bf16),
            pltpu.SemaphoreType.DMA((COPIES,)),
            pltpu.SemaphoreType.DMA((COPIES,)),
            pltpu.SemaphoreType.DMA((5,)),
        ],
        compiler_params=pltpu.CompilerParams(
            collective_id=0, has_side_effects=True, vmem_limit_bytes=56 * 1024 * 1024
        ),
        cost_estimate=pl.CostEstimate(flops=6_442_450_944, bytes_accessed=3_000_000, transcendentals=0),
        name="hyena_block",
    )(tokens, value_weight, key_gate, query_gate, conv_filter, out_weight)


def solution(mesh):
    return jax.shard_map(
        on_device,
        mesh=mesh,
        in_specs=(
            P("tok", "ch"),
            P("tok", "ch"),
            P("tok", "ch"),
            P("tok", "ch"),
            P("ch", None),
            P("tok", "ch"),
        ),
        out_specs=P("tok", "ch"),
        check_vma=False,
    )
```

```python
import functools

import jax
import jax.numpy as jnp
from jax import lax
from jax.experimental import pallas as pl
from jax.experimental.pallas import tpu as pltpu
from jax.sharding import PartitionSpec as P

MESH = pl.DeviceIdType.MESH
TAPS = 128
GROUP = 16
ROWS = 384
WIDTH = 512
HALF = WIDTH // 2
RELAY = 16
CHUNKS = (((0, 192), (192, 192)), ((128, 128), (256, 128), (0, 128)))
WHOLE = (0, ROWS)


class Names:
    def __init__(self):
        self.index = {}

    def __call__(self, name):
        return self.index.setdefault(name, len(self.index))


def place(x, y, z, c):
    return (x * 4 + (z // 4) * 2 + c, y * 4 + lax.rem(z, 4))


def kernel(
    tok_hbm, wv_hbm, key_hbm, query_hbm, filt_ref, wo_hbm,
    out_ref,
    wbuf_v, wbuf_o, tbuf_v, tbuf_o, band, base, ext, key, query,
    acc_away, acc_own, part_out, part_in, send_sem, recv_sem, local_sem,
):
    tok = lax.axis_index("tok")
    ch = lax.axis_index("ch")
    x, zh, c = tok // 4, lax.rem(tok // 2, 2), lax.rem(tok, 2)
    y, zl = ch // 4, lax.rem(ch, 4)
    zl1, zl0 = zl // 2, lax.rem(zl, 2)
    z = zh * 4 + zl
    master = c == zl0
    nm = jnp.logical_not(master)

    def near(zl0_):
        return zh * 4 + zl1 * 2 + zl0_

    xp, xm, x2 = lax.rem(x + 1, 4), lax.rem(x + 3, 4), lax.rem(x + 2, 4)
    yp, ym, y2 = lax.rem(y + 1, 4), lax.rem(y + 3, 4), lax.rem(y + 2, 4)
    dev_xp, dev_xm = place(xp, y, z, c), place(xm, y, z, c)
    dev_yp, dev_ym = place(x, yp, z, c), place(x, ym, z, c)
    dev_z1 = place(x, y, near(1 - zl0), c)
    dev_z2 = place(x, y, zh * 4 + (1 - zl1) * 2 + zl0, c)
    far_zl0 = jnp.where(master, zl0, 1 - zl0)
    dev_far = place(x, y, (1 - zh) * 4 + zl1 * 2 + far_zl0, jnp.where(master, c, 1 - c))
    dev_sib = place(x, y, z, 1 - c)
    dev_next = (lax.rem(tok + 1, 16), ch)
    dev_prev = (lax.rem(tok + 15, 16), ch)
    dev_other = (jnp.where(c == 1, lax.rem(tok + 1, 16), lax.rem(tok + 15, 16)), ch)

    barrier = pltpu.get_barrier_semaphore()
    partners = (dev_xp, dev_xm, dev_yp, dev_ym, dev_z1, dev_z2, dev_far, dev_sib, dev_other)
    for d in partners:
        pl.semaphore_signal(barrier, inc=1, device_id=d, device_id_type=MESH)
    pl.semaphore_wait(barrier, len(partners))

    w_hbm = (wv_hbm, wo_hbm)
    wbuf = (wbuf_v, wbuf_o)
    tbuf = (tbuf_v, tbuf_o)
    own, away = zl0, 1 - zl0
    names = Names()

    def slot(b, zz, j):
        return b * 8 + zz * 4 + j

    root_z = jnp.where(master, zh, 1 - zh)
    root_b = (jnp.where(master, own, away), jnp.where(master, away, own))

    sent = {}
    role = ["all"]

    class Sent:
        def __init__(self, name, src, dst, dev):
            i = names(name)
            self.name = name
            self.make = lambda: pltpu.make_async_remote_copy(
                src_ref=src, dst_ref=dst, send_sem=send_sem.at[i], recv_sem=recv_sem.at[i],
                device_id=dev, device_id_type=MESH,
            )

        def start(self):
            sent.setdefault(self.name, set()).add(role[0])
            self.make().start()

        def wait_recv(self):
            self.make().wait_recv()

        def wait_send(self):
            self.make().wait_send()

    copy = Sent

    def when_master(body):
        role[0] = "master"
        pl.when(master)(body)
        role[0] = "all"

    def when_not(body):
        role[0] = "nm"
        pl.when(nm)(body)
        role[0] = "all"

    def half(h):
        return pl.ds(h * HALF, HALF)

    def w_in(m, h, recv=False):
        s = slot(away if recv else own, zh, x)
        return copy(("in", m, h), w_hbm[m].at[half(h)], wbuf[m].at[s, half(h)], dev_z1)

    def w_far(m, h, recv=False):
        s = slot(away, 1 - zh, x) if recv else slot(own, zh, x)
        return copy(("far", m, h), w_hbm[m].at[half(h)], wbuf[m].at[s, half(h)], dev_far)

    def w_pre(m, h):
        return copy(("pre", m, h), w_hbm[m].at[half(h)], wbuf[m].at[RELAY, half(h)], dev_z1)

    def w_anti(m, h, recv=False):
        s = slot(own, 1 - zh, x) if recv else slot(away, zh, x)
        return copy(("anti", m, h), wbuf[m].at[RELAY, half(h)], wbuf[m].at[s, half(h)], dev_far)

    def w_x(m, r, way, h, recv=False, native=False):
        from_x = (xm if way > 0 else xp) if recv else x
        dst = wbuf[m].at[slot(root_b[r], root_z, from_x), half(h)]
        src = w_hbm[m].at[half(h)] if native else dst
        return copy(("x", m, r, way, h), src, dst, dev_xp if way > 0 else dev_xm)

    def w_fwd(m, r, way, recv=False):
        from_x = x2 if recv else (xm if way > 0 else xp)
        s = wbuf[m].at[slot(root_b[r], root_z, from_x), half(first_half(way))]
        return copy(("fwd", m, r, way), s, s, dev_xp if way > 0 else dev_xm)

    def w_sib(m, r, k, recv=False, native=False):
        j = (x, xm, xp, x2)[k]
        s = slot(1 - root_b[r], 1 - root_z, j) if recv else slot(root_b[r], root_z, j)
        src = w_hbm[m] if native else wbuf[m].at[s]
        return copy(("sib", m, r, k), src, wbuf[m].at[s], dev_sib)

    def first_half(way):
        return 0 if way > 0 else 1

    def t_y(q, ch_, p, way, h, recv=False):
        first, n = CHUNKS[q][ch_]
        from_y = (ym if way > 0 else yp) if recv else y
        k = (zl1 if p == 0 else 1 - zl1) * 4 + from_y
        rows = pl.ds(first + h * (n // 2), n // 2)
        ref = tbuf[q].at[k, rows]
        src = tok_hbm.at[rows] if q == 0 and p == 0 else ref
        return copy(("ty", q, ch_, p, way, h), src, ref, dev_yp if way > 0 else dev_ym)

    def t_fwd(q, ch_, p, way, recv=False):
        first, n = CHUNKS[q][ch_]
        from_y = y2 if recv else (ym if way > 0 else yp)
        k = (zl1 if p == 0 else 1 - zl1) * 4 + from_y
        ref = tbuf[q].at[k, pl.ds(first + first_half(way) * (n // 2), n // 2)]
        return copy(("tfwd", q, ch_, p, way), ref, ref, dev_yp if way > 0 else dev_ym)

    def t_far(q, ch_, recv=False):
        first, n = CHUNKS[q][ch_]
        ref = tbuf[q].at[((1 - zl1) if recv else zl1) * 4 + y, pl.ds(first, n)]
        src = tok_hbm.at[pl.ds(first, n)] if q == 0 else ref
        return copy(("tz", q, ch_), src, ref, dev_z2)

    def partial(q, ch_):
        rows = pl.ds(*(WHOLE if q == 0 else CHUNKS[1][ch_]))
        return copy(("c", q, ch_), part_out.at[q, rows], part_in.at[q, rows], dev_z1)

    def halo():
        return copy(("halo",), ext.at[pl.ds(ROWS, TAPS)], ext.at[pl.ds(0, TAPS)], dev_next)

    senders = {
        "in": w_in, "far": w_far, "pre": w_pre, "anti": w_anti, "x": w_x, "fwd": w_fwd, "sib": w_sib,
        "ty": t_y, "tfwd": t_fwd, "tz": t_far, "c": partial, "halo": halo,
    }

    def send_x(m, r, native=False):
        for h in range(2):
            for way in (1, -1):
                w_x(m, r, way, h if way > 0 else 1 - h, native=native).start()

    def relay_x(m, r):
        for way in (1, -1):
            w_x(m, r, way, first_half(way), recv=True).wait_recv()
            w_fwd(m, r, way).start()

    def mid_x(m, r):
        for way in (1, -1):
            w_x(m, r, way, 1 - first_half(way), recv=True).wait_recv()
        w_sib(m, r, 1).start()
        w_sib(m, r, 2).start()

    def end_x(m, r):
        for way in (1, -1):
            w_fwd(m, r, way, recv=True).wait_recv()
        w_sib(m, r, 3).start()

    def take_half(m, r, h, arrival):
        arrival(m, h, recv=True).wait_recv()
        for way in (1, -1):
            w_x(m, r, way, h).start()
        if h == 1:
            w_sib(m, r, 0).start()

    def send_y(q, ch_, p):
        for h in range(2):
            for way in (1, -1):
                t_y(q, ch_, p, way, h if way > 0 else 1 - h).start()

    def relay_y(q, ch_, p):
        for way in (1, -1):
            t_y(q, ch_, p, way, first_half(way), recv=True).wait_recv()
            t_fwd(q, ch_, p, way).start()

    def end_y(q, ch_, p):
        for way in (1, -1):
            t_y(q, ch_, p, way, 1 - first_half(way), recv=True).wait_recv()
            t_fwd(q, ch_, p, way, recv=True).wait_recv()

    def far_y(q, ch_):
        t_far(q, ch_, recv=True).wait_recv()
        send_y(q, ch_, 1)

    def z_in(m, h):
        w_in(m, h).start()

    def z_far(m, h):
        w_far(m, h).start()

    def z_pre(m, h):
        w_pre(m, h).start()

    def pass_on(m, h):
        w_pre(m, h).wait_recv()
        w_anti(m, h).start()

    def t_z(ch_):
        t_far(0, ch_).start()

    def x_master(m):
        send_x(m, 0, native=True)
        w_sib(m, 0, 0, native=True).start()

    def local(i, src, dst):
        return pltpu.make_async_copy(src, dst, local_sem.at[i])

    def own_w(m):
        return local(m, w_hbm[m], wbuf[m].at[slot(own, zh, x)])


    @when_not
    def _():
        z_far(0, 0)
        z_in(0, 0)


    @when_master
    def _():
        x_master(0)


    own_tok = local(2, tok_hbm, tbuf[0].at[zl1 * 4 + y])
    own_key = local(3, key_hbm, key)
    own_query = local(4, query_hbm, query)
    own_tok.start()
    own_key.start()
    own_query.start()

    @when_master
    def _():
        own_w(0).start()
        own_w(1).start()

    s_at = lax.broadcasted_iota(jnp.int32, (TAPS, 2 * TAPS), 1)
    j_at = lax.broadcasted_iota(jnp.int32, (TAPS, 2 * TAPS), 0)
    flip = jnp.where(s_at + j_at == TAPS, 1.0, 0.0).astype(jnp.bfloat16)
    base[...] = jnp.dot(filt_ref[...].astype(jnp.bfloat16), flip, preferred_element_type=jnp.float32)

    @pl.loop(0, WIDTH // GROUP)
    def _(g):
        rows = jnp.broadcast_to(base[pl.ds(g, 1), :], (TAPS, 2 * TAPS))
        turned = pltpu.roll(rows, 0, 1, stride=1, stride_axis=0)
        band[pl.ds(pl.multiple_of(g * TAPS, TAPS), TAPS), :] = turned.astype(jnp.bfloat16)

    acc_away[...] = jnp.zeros_like(acc_away)
    acc_own[...] = jnp.zeros_like(acc_own)

    def multiply(q, acc, rows, b, zz):
        for n in range(2):
            cols = pl.ds(n * 256, 256)
            total = None
            for j in range(4):
                term = jnp.dot(
                    tbuf[q][zz * 4 + j, rows, :],
                    wbuf[q][slot(b, zz, j), :, cols],
                    preferred_element_type=jnp.float32,
                )
                total = term if total is None else total + term
            acc[rows, cols] += total

    def wait_sib(m, r):
        for k in range(4):
            w_sib(m, r, k, recv=True).wait_recv()

    every = pl.ds(0, ROWS)
    k_own = zl1 * 4 + y

    def convolve(blocks):
        width = len(blocks) * TAPS
        lane_group = lax.rem(lax.broadcasted_iota(jnp.int32, (TAPS, width), 1), TAPS) // GROUP
        for tile in range(WIDTH // TAPS):
            lanes = pl.ds(tile * TAPS, TAPS)
            parts = [ext[pl.ds(block * TAPS, 2 * TAPS), lanes] for block in blocks]
            window = parts[0] if len(parts) == 1 else jnp.concatenate(parts, axis=1)
            conv = None
            for g in range(8):
                raw = jnp.dot(
                    band[pl.ds((tile * 8 + g) * TAPS, TAPS), :], window, preferred_element_type=jnp.float32
                )
                conv = raw if conv is None else jnp.where(lane_group == g, raw, conv)
            for i, block in enumerate(blocks):
                rows = pl.ds(block * TAPS, TAPS)
                shaped = conv[:, i * TAPS : (i + 1) * TAPS] * query[rows, lanes].astype(jnp.float32)
                tbuf_o[k_own, rows, lanes] = shaped.astype(jnp.bfloat16)

    def send_shaped(ch_):
        t_far(1, ch_).start()
        send_y(1, ch_, 0)

    def away0():
        own_tok.wait()

        @pl.when(master)
        def _():
            own_w(0).wait()
            own_w(1).wait()

        for zz in range(2):
            multiply(0, acc_away, every, away, zz)
        part_out[0] = acc_away[...].astype(jnp.bfloat16)
        partial(0, 0).start()
        acc_away[...] = jnp.zeros_like(acc_away)

    def own0(zz):
        multiply(0, acc_own, every, own, zz)

    def gate():
        own_key.wait()
        own_query.wait()
        partial(0, 0).wait_recv()
        values = (acc_own[...] + part_in[0].astype(jnp.float32)).astype(jnp.bfloat16)
        ext[pl.ds(TAPS, ROWS), :] = (values.astype(jnp.float32) * key[...].astype(jnp.float32)).astype(jnp.bfloat16)
        halo().start()
        convolve((1, 2))
        send_shaped(0)
        send_shaped(1)
        acc_own[...] = jnp.zeros_like(acc_own)

    def rim():
        halo().wait_recv()

        @pl.when(tok == 0)
        def _():
            ext[pl.ds(0, TAPS), :] = jnp.zeros((TAPS, WIDTH), jnp.bfloat16)

        convolve((0,))
        send_shaped(2)

    def near2(ch_):
        rows = pl.ds(*CHUNKS[1][ch_])
        multiply(1, acc_away, rows, away, zl1)
        multiply(1, acc_own, rows, own, zl1)

    def far2(ch_):
        rows = pl.ds(*CHUNKS[1][ch_])
        multiply(1, acc_away, rows, away, 1 - zl1)
        part_out[1, rows] = acc_away[rows].astype(jnp.bfloat16)
        partial(1, ch_).start()
        multiply(1, acc_own, rows, own, 1 - zl1)

    def result(ch_):
        rows = pl.ds(*CHUNKS[1][ch_])
        partial(1, ch_).wait_recv()
        out_ref[rows] = (acc_own[rows] + part_in[1, rows].astype(jnp.float32)).astype(jnp.bfloat16)


    @when_master
    def _():
        relay_x(0, 0)
        take_half(0, 1, 0, w_in)
        x_master(1)
        z_pre(0, 0)
        send_y(0, 0, 0)
        relay_y(0, 0, 0)
        take_half(0, 1, 1, w_in)
        t_z(0)
        relay_x(0, 1)
        z_pre(0, 1)
        t_z(1)
        relay_x(1, 0)
        end_y(0, 0, 0)
        z_pre(1, 0)
        far_y(0, 0)
        end_x(0, 0)
        far_y(0, 1)
        mid_x(0, 1)
        end_x(0, 1)
        z_pre(1, 1)
        relay_y(0, 1, 1)
        mid_x(0, 0)
        send_y(0, 1, 0)
        relay_y(0, 0, 1)
        end_y(0, 1, 1)
        take_half(1, 1, 0, w_in)
        mid_x(1, 0)
        relay_y(0, 1, 0)
        end_y(0, 0, 1)
        end_y(0, 1, 0)
        take_half(1, 1, 1, w_in)
        end_x(1, 0)
        wait_sib(0, 0)


    @when_not
    def _():
        z_far(0, 1)
        t_z(0)
        send_y(0, 0, 0)
        relay_y(0, 0, 0)
        z_in(0, 1)
        t_z(1)
        end_y(0, 0, 0)
        z_in(1, 1)
        far_y(0, 1)
        take_half(0, 0, 0, w_far)
        send_y(0, 1, 0)
        far_y(0, 0)
        pass_on(0, 0)
        pass_on(0, 1)
        take_half(0, 0, 1, w_far)
        relay_y(0, 1, 1)
        z_far(1, 0)
        relay_y(0, 0, 1)
        relay_x(0, 0)
        mid_x(0, 0)
        end_y(0, 1, 1)
        relay_y(0, 1, 0)
        take_half(0, 1, 0, w_anti)
        end_x(0, 0)
        end_y(0, 0, 1)
        z_in(1, 0)
        wait_sib(0, 1)
        end_y(0, 1, 0)
        take_half(0, 1, 1, w_anti)
        z_far(1, 1)

    away0()

    @when_master
    def _():
        wait_sib(0, 1)


    @when_not
    def _():
        wait_sib(0, 0)

    own0(zh)

    @when_master
    def _():
        relay_x(1, 1)


    @when_not
    def _():
        relay_x(0, 1)
        mid_x(0, 1)
        take_half(1, 0, 0, w_far)
        end_x(0, 1)
        pass_on(1, 1)
        take_half(1, 0, 1, w_far)
        pass_on(1, 0)

    own0(1 - zh)
    gate()

    @when_master
    def _():
        far_y(1, 0)
        mid_x(1, 1)
        end_x(1, 1)

    rim()

    @when_master
    def _():
        relay_y(1, 0, 0)
        relay_y(1, 1, 0)
        far_y(1, 1)
        relay_y(1, 0, 1)
        end_y(1, 0, 0)
        relay_y(1, 2, 0)
        relay_y(1, 1, 1)
        end_y(1, 2, 0)
        end_y(1, 1, 0)
        wait_sib(1, 0)
        far_y(1, 2)
        wait_sib(1, 1)


    @when_not
    def _():
        take_half(1, 1, 0, w_anti)
        relay_y(1, 0, 0)
        relay_x(1, 0)
        take_half(1, 1, 1, w_anti)
        relay_y(1, 1, 0)
        relay_y(1, 2, 0)
        far_y(1, 0)
        end_x(1, 0)
        relay_x(1, 1)
        mid_x(1, 1)
        end_y(1, 1, 0)
        end_y(1, 0, 0)
        far_y(1, 1)
        mid_x(1, 0)
        relay_y(1, 0, 1)
        wait_sib(1, 0)
        relay_y(1, 1, 1)
        far_y(1, 2)
        end_x(1, 1)
        wait_sib(1, 1)

    near2(0)

    @when_master
    def _():
        end_y(1, 0, 1)


    @when_not
    def _():
        end_y(1, 2, 0)

    near2(1)

    @when_not
    def _():
        end_y(1, 0, 1)

    far2(0)

    @when_master
    def _():
        end_y(1, 1, 1)
        relay_y(1, 2, 1)


    @when_not
    def _():
        end_y(1, 1, 1)

    far2(1)

    @when_not
    def _():
        relay_y(1, 2, 1)

    near2(2)

    @when_master
    def _():
        end_y(1, 2, 1)


    @when_not
    def _():
        end_y(1, 2, 1)

    far2(2)
    result(0)
    result(2)
    result(1)

    def last(only):
        for name, roles in sent.items():
            if ("all" in roles or len(roles) == 2) == (only == "all") and (only == "all" or only in roles):
                senders[name[0]](*name[1:]).wait_send()

    last("all")

    @when_master
    def _():
        last("master")

    @when_not
    def _():
        last("nm")


COPIES = 144


def on_device(tokens, value_weight, key_gate, query_gate, conv_filter, out_weight):
    hbm = pl.BlockSpec(memory_space=pl.ANY)
    vmem = pl.BlockSpec(memory_space=pltpu.VMEM)
    bf16, f32 = jnp.bfloat16, jnp.float32
    return pl.pallas_call(
        kernel,
        out_shape=jax.ShapeDtypeStruct((ROWS, WIDTH), bf16),
        in_specs=[hbm, hbm, hbm, hbm, vmem, hbm],
        out_specs=vmem,
        scratch_shapes=[
            pltpu.VMEM((17, WIDTH, WIDTH), bf16),
            pltpu.VMEM((17, WIDTH, WIDTH), bf16),
            pltpu.VMEM((8, ROWS, WIDTH), bf16),
            pltpu.VMEM((8, ROWS, WIDTH), bf16),
            pltpu.VMEM((WIDTH // GROUP * TAPS, 2 * TAPS), bf16),
            pltpu.VMEM((WIDTH // GROUP, 2 * TAPS), f32),
            pltpu.VMEM((TAPS + ROWS, WIDTH), bf16),
            pltpu.VMEM((ROWS, WIDTH), bf16),
            pltpu.VMEM((ROWS, WIDTH), bf16),
            pltpu.VMEM((ROWS, WIDTH), f32),
            pltpu.VMEM((ROWS, WIDTH), f32),
            pltpu.VMEM((2, ROWS, WIDTH), bf16),
            pltpu.VMEM((2, ROWS, WIDTH), bf16),
            pltpu.SemaphoreType.DMA((COPIES,)),
            pltpu.SemaphoreType.DMA((COPIES,)),
            pltpu.SemaphoreType.DMA((5,)),
        ],
        compiler_params=pltpu.CompilerParams(
            collective_id=0, has_side_effects=True, vmem_limit_bytes=56 * 1024 * 1024
        ),
        cost_estimate=pl.CostEstimate(flops=6_442_450_944, bytes_accessed=3_000_000, transcendentals=0),
        name="hyena_block",
    )(tokens, value_weight, key_gate, query_gate, conv_filter, out_weight)


def solution(mesh):
    return jax.shard_map(
        on_device,
        mesh=mesh,
        in_specs=(
            P("tok", "ch"),
            P("tok", "ch"),
            P("tok", "ch"),
            P("tok", "ch"),
            P("ch", None),
            P("tok", "ch"),
        ),
        out_specs=P("tok", "ch"),
        check_vma=False,
    )
```

```python
import functools

import jax
import jax.numpy as jnp
from jax import lax
from jax.experimental import pallas as pl
from jax.experimental.pallas import tpu as pltpu
from jax.sharding import PartitionSpec as P

MESH = pl.DeviceIdType.MESH
TAPS = 128
GROUP = 16
ROWS = 384
WIDTH = 512
HALF = WIDTH // 2
RELAY = 16
CHUNKS = (((0, 192), (192, 192)), ((128, 128), (256, 128), (0, 128)))
WHOLE = (0, ROWS)


class Names:
    def __init__(self):
        self.index = {}

    def __call__(self, name):
        return self.index.setdefault(name, len(self.index))


def place(x, y, z, c):
    return (x * 4 + (z // 4) * 2 + c, y * 4 + lax.rem(z, 4))


def kernel(
    tok_hbm, wv_hbm, key_hbm, query_hbm, filt_ref, wo_hbm,
    out_ref,
    wbuf_v, wbuf_o, tbuf_v, tbuf_o, band, base, ext, key, query,
    acc_away, acc_own, part_out, part_in, send_sem, recv_sem, local_sem,
):
    tok = lax.axis_index("tok")
    ch = lax.axis_index("ch")
    x, zh, c = tok // 4, lax.rem(tok // 2, 2), lax.rem(tok, 2)
    y, zl = ch // 4, lax.rem(ch, 4)
    zl1, zl0 = zl // 2, lax.rem(zl, 2)
    z = zh * 4 + zl
    master = c == zl0
    nm = jnp.logical_not(master)

    def near(zl0_):
        return zh * 4 + zl1 * 2 + zl0_

    xp, xm, x2 = lax.rem(x + 1, 4), lax.rem(x + 3, 4), lax.rem(x + 2, 4)
    yp, ym, y2 = lax.rem(y + 1, 4), lax.rem(y + 3, 4), lax.rem(y + 2, 4)
    dev_xp, dev_xm = place(xp, y, z, c), place(xm, y, z, c)
    dev_yp, dev_ym = place(x, yp, z, c), place(x, ym, z, c)
    dev_z1 = place(x, y, near(1 - zl0), c)
    dev_z2 = place(x, y, zh * 4 + (1 - zl1) * 2 + zl0, c)
    far_zl0 = jnp.where(master, zl0, 1 - zl0)
    dev_far = place(x, y, (1 - zh) * 4 + zl1 * 2 + far_zl0, jnp.where(master, c, 1 - c))
    dev_sib = place(x, y, z, 1 - c)
    dev_next = (lax.rem(tok + 1, 16), ch)
    dev_prev = (lax.rem(tok + 15, 16), ch)
    dev_other = (jnp.where(c == 1, lax.rem(tok + 1, 16), lax.rem(tok + 15, 16)), ch)

    barrier = pltpu.get_barrier_semaphore()
    partners = (dev_xp, dev_xm, dev_yp, dev_ym, dev_z1, dev_z2, dev_far, dev_sib, dev_other)
    for d in partners:
        pl.semaphore_signal(barrier, inc=1, device_id=d, device_id_type=MESH)
    pl.semaphore_wait(barrier, len(partners))

    w_hbm = (wv_hbm, wo_hbm)
    wbuf = (wbuf_v, wbuf_o)
    tbuf = (tbuf_v, tbuf_o)
    own, away = zl0, 1 - zl0
    names = Names()

    def slot(b, zz, j):
        return b * 8 + zz * 4 + j

    root_z = jnp.where(master, zh, 1 - zh)
    root_b = (jnp.where(master, own, away), jnp.where(master, away, own))

    sent = {}
    role = ["all"]

    class Sent:
        def __init__(self, name, src, dst, dev):
            i = names(name)
            self.name = name
            self.make = lambda: pltpu.make_async_remote_copy(
                src_ref=src, dst_ref=dst, send_sem=send_sem.at[i], recv_sem=recv_sem.at[i],
                device_id=dev, device_id_type=MESH,
            )

        def start(self):
            sent.setdefault(self.name, set()).add(role[0])
            self.make().start()

        def wait_recv(self):
            self.make().wait_recv()

        def wait_send(self):
            self.make().wait_send()

    copy = Sent

    def when_master(body):
        role[0] = "master"
        pl.when(master)(body)
        role[0] = "all"

    def when_not(body):
        role[0] = "nm"
        pl.when(nm)(body)
        role[0] = "all"

    def half(h):
        return pl.ds(h * HALF, HALF)

    def w_in(m, h, recv=False):
        s = slot(away if recv else own, zh, x)
        return copy(("in", m, h), w_hbm[m].at[half(h)], wbuf[m].at[s, half(h)], dev_z1)

    def w_far(m, h, recv=False):
        s = slot(away, 1 - zh, x) if recv else slot(own, zh, x)
        return copy(("far", m, h), w_hbm[m].at[half(h)], wbuf[m].at[s, half(h)], dev_far)

    def w_pre(m, h):
        return copy(("pre", m, h), w_hbm[m].at[half(h)], wbuf[m].at[RELAY, half(h)], dev_z1)

    def w_anti(m, h, recv=False):
        s = slot(own, 1 - zh, x) if recv else slot(away, zh, x)
        return copy(("anti", m, h), wbuf[m].at[RELAY, half(h)], wbuf[m].at[s, half(h)], dev_far)

    def w_x(m, r, way, h, recv=False, native=False):
        from_x = (xm if way > 0 else xp) if recv else x
        dst = wbuf[m].at[slot(root_b[r], root_z, from_x), half(h)]
        src = w_hbm[m].at[half(h)] if native else dst
        return copy(("x", m, r, way, h), src, dst, dev_xp if way > 0 else dev_xm)

    def w_fwd(m, r, way, recv=False):
        from_x = x2 if recv else (xm if way > 0 else xp)
        s = wbuf[m].at[slot(root_b[r], root_z, from_x), half(first_half(way))]
        return copy(("fwd", m, r, way), s, s, dev_xp if way > 0 else dev_xm)

    def w_sib(m, r, k, recv=False, native=False):
        j = (x, xm, xp, x2)[k]
        s = slot(1 - root_b[r], 1 - root_z, j) if recv else slot(root_b[r], root_z, j)
        src = w_hbm[m] if native else wbuf[m].at[s]
        return copy(("sib", m, r, k), src, wbuf[m].at[s], dev_sib)

    def first_half(way):
        return 0 if way > 0 else 1

    def t_y(q, ch_, p, way, h, recv=False):
        first, n = CHUNKS[q][ch_]
        from_y = (ym if way > 0 else yp) if recv else y
        k = (zl1 if p == 0 else 1 - zl1) * 4 + from_y
        rows = pl.ds(first + h * (n // 2), n // 2)
        ref = tbuf[q].at[k, rows]
        src = tok_hbm.at[rows] if q == 0 and p == 0 else ref
        return copy(("ty", q, ch_, p, way, h), src, ref, dev_yp if way > 0 else dev_ym)

    def t_fwd(q, ch_, p, way, recv=False):
        first, n = CHUNKS[q][ch_]
        from_y = y2 if recv else (ym if way > 0 else yp)
        k = (zl1 if p == 0 else 1 - zl1) * 4 + from_y
        ref = tbuf[q].at[k, pl.ds(first + first_half(way) * (n // 2), n // 2)]
        return copy(("tfwd", q, ch_, p, way), ref, ref, dev_yp if way > 0 else dev_ym)

    def t_far(q, ch_, recv=False):
        first, n = CHUNKS[q][ch_]
        ref = tbuf[q].at[((1 - zl1) if recv else zl1) * 4 + y, pl.ds(first, n)]
        src = tok_hbm.at[pl.ds(first, n)] if q == 0 else ref
        return copy(("tz", q, ch_), src, ref, dev_z2)

    def partial(q, ch_):
        rows = pl.ds(*(WHOLE if q == 0 else CHUNKS[1][ch_]))
        return copy(("c", q, ch_), part_out.at[q, rows], part_in.at[q, rows], dev_z1)

    def halo():
        return copy(("halo",), ext.at[pl.ds(ROWS, TAPS)], ext.at[pl.ds(0, TAPS)], dev_next)

    senders = {
        "in": w_in, "far": w_far, "pre": w_pre, "anti": w_anti, "x": w_x, "fwd": w_fwd, "sib": w_sib,
        "ty": t_y, "tfwd": t_fwd, "tz": t_far, "c": partial, "halo": halo,
    }

    def send_x(m, r, native=False):
        for h in range(2):
            for way in (1, -1):
                w_x(m, r, way, h if way > 0 else 1 - h, native=native).start()

    def relay_x(m, r):
        for way in (1, -1):
            w_x(m, r, way, first_half(way), recv=True).wait_recv()
            w_fwd(m, r, way).start()

    def mid_x(m, r):
        for way in (1, -1):
            w_x(m, r, way, 1 - first_half(way), recv=True).wait_recv()
        w_sib(m, r, 1).start()
        w_sib(m, r, 2).start()

    def end_x(m, r):
        for way in (1, -1):
            w_fwd(m, r, way, recv=True).wait_recv()
        w_sib(m, r, 3).start()

    def take_half(m, r, h, arrival):
        arrival(m, h, recv=True).wait_recv()
        for way in (1, -1):
            w_x(m, r, way, h).start()
        if h == 1:
            w_sib(m, r, 0).start()

    def send_y(q, ch_, p):
        for h in range(2):
            for way in (1, -1):
                t_y(q, ch_, p, way, h if way > 0 else 1 - h).start()

    def relay_y(q, ch_, p):
        for way in (1, -1):
            t_y(q, ch_, p, way, first_half(way), recv=True).wait_recv()
            t_fwd(q, ch_, p, way).start()

    def end_y(q, ch_, p):
        for way in (1, -1):
            t_y(q, ch_, p, way, 1 - first_half(way), recv=True).wait_recv()
            t_fwd(q, ch_, p, way, recv=True).wait_recv()

    def far_y(q, ch_):
        t_far(q, ch_, recv=True).wait_recv()
        send_y(q, ch_, 1)

    def z_in(m, h):
        w_in(m, h).start()

    def z_far(m, h):
        w_far(m, h).start()

    def z_pre(m, h):
        w_pre(m, h).start()

    def pass_on(m, h):
        w_pre(m, h).wait_recv()
        w_anti(m, h).start()

    def t_z(ch_):
        t_far(0, ch_).start()

    def x_master(m):
        send_x(m, 0, native=True)
        w_sib(m, 0, 0, native=True).start()

    def local(i, src, dst):
        return pltpu.make_async_copy(src, dst, local_sem.at[i])

    def own_w(m):
        return local(m, w_hbm[m], wbuf[m].at[slot(own, zh, x)])


    @when_not
    def _():
        z_far(0, 0)


    @when_master
    def _():
        send_y(0, 0, 0)


    @when_not
    def _():
        z_in(0, 0)


    @when_master
    def _():
        x_master(0)


    own_tok = local(2, tok_hbm, tbuf[0].at[zl1 * 4 + y])
    own_key = local(3, key_hbm, key)
    own_query = local(4, query_hbm, query)
    own_tok.start()
    own_key.start()
    own_query.start()

    @when_master
    def _():
        own_w(0).start()
        own_w(1).start()

    s_at = lax.broadcasted_iota(jnp.int32, (TAPS, 2 * TAPS), 1)
    j_at = lax.broadcasted_iota(jnp.int32, (TAPS, 2 * TAPS), 0)
    flip = jnp.where(s_at + j_at == TAPS, 1.0, 0.0).astype(jnp.bfloat16)
    base[...] = jnp.dot(filt_ref[...].astype(jnp.bfloat16), flip, preferred_element_type=jnp.float32)

    @pl.loop(0, WIDTH // GROUP)
    def _(g):
        rows = jnp.broadcast_to(base[pl.ds(g, 1), :], (TAPS, 2 * TAPS))
        turned = pltpu.roll(rows, 0, 1, stride=1, stride_axis=0)
        band[pl.ds(pl.multiple_of(g * TAPS, TAPS), TAPS), :] = turned.astype(jnp.bfloat16)

    acc_away[...] = jnp.zeros_like(acc_away)
    acc_own[...] = jnp.zeros_like(acc_own)

    def multiply(q, acc, rows, b, zz):
        for n in range(2):
            cols = pl.ds(n * 256, 256)
            total = None
            for j in range(4):
                term = jnp.dot(
                    tbuf[q][zz * 4 + j, rows, :],
                    wbuf[q][slot(b, zz, j), :, cols],
                    preferred_element_type=jnp.float32,
                )
                total = term if total is None else total + term
            acc[rows, cols] += total

    def wait_sib(m, r):
        for k in range(4):
            w_sib(m, r, k, recv=True).wait_recv()

    every = pl.ds(0, ROWS)
    k_own = zl1 * 4 + y

    def convolve(blocks):
        width = len(blocks) * TAPS
        lane_group = lax.rem(lax.broadcasted_iota(jnp.int32, (TAPS, width), 1), TAPS) // GROUP
        for tile in range(WIDTH // TAPS):
            lanes = pl.ds(tile * TAPS, TAPS)
            parts = [ext[pl.ds(block * TAPS, 2 * TAPS), lanes] for block in blocks]
            window = parts[0] if len(parts) == 1 else jnp.concatenate(parts, axis=1)
            conv = None
            for g in range(8):
                raw = jnp.dot(
                    band[pl.ds((tile * 8 + g) * TAPS, TAPS), :], window, preferred_element_type=jnp.float32
                )
                conv = raw if conv is None else jnp.where(lane_group == g, raw, conv)
            for i, block in enumerate(blocks):
                rows = pl.ds(block * TAPS, TAPS)
                shaped = conv[:, i * TAPS : (i + 1) * TAPS] * query[rows, lanes].astype(jnp.float32)
                tbuf_o[k_own, rows, lanes] = shaped.astype(jnp.bfloat16)

    def send_shaped(ch_):
        t_far(1, ch_).start()
        send_y(1, ch_, 0)

    def away0():
        own_tok.wait()

        @pl.when(master)
        def _():
            own_w(0).wait()
            own_w(1).wait()

        for zz in range(2):
            multiply(0, acc_away, every, away, zz)
        part_out[0] = acc_away[...].astype(jnp.bfloat16)
        partial(0, 0).start()
        acc_away[...] = jnp.zeros_like(acc_away)

    def own0(zz):
        multiply(0, acc_own, every, own, zz)

    def gate():
        own_key.wait()
        own_query.wait()
        partial(0, 0).wait_recv()
        values = (acc_own[...] + part_in[0].astype(jnp.float32)).astype(jnp.bfloat16)
        ext[pl.ds(TAPS, ROWS), :] = (values.astype(jnp.float32) * key[...].astype(jnp.float32)).astype(jnp.bfloat16)
        halo().start()
        convolve((1, 2))
        send_shaped(0)
        send_shaped(1)
        acc_own[...] = jnp.zeros_like(acc_own)

    def rim():
        halo().wait_recv()

        @pl.when(tok == 0)
        def _():
            ext[pl.ds(0, TAPS), :] = jnp.zeros((TAPS, WIDTH), jnp.bfloat16)

        convolve((0,))
        send_shaped(2)

    def near2(ch_):
        rows = pl.ds(*CHUNKS[1][ch_])
        multiply(1, acc_away, rows, away, zl1)
        multiply(1, acc_own, rows, own, zl1)

    def far2(ch_):
        rows = pl.ds(*CHUNKS[1][ch_])
        multiply(1, acc_away, rows, away, 1 - zl1)
        part_out[1, rows] = acc_away[rows].astype(jnp.bfloat16)
        partial(1, ch_).start()
        multiply(1, acc_own, rows, own, 1 - zl1)

    def result(ch_):
        rows = pl.ds(*CHUNKS[1][ch_])
        partial(1, ch_).wait_recv()
        out_ref[rows] = (acc_own[rows] + part_in[1, rows].astype(jnp.float32)).astype(jnp.bfloat16)


    @when_master
    def _():
        relay_x(0, 0)
        take_half(0, 1, 0, w_in)
        z_pre(0, 0)
        x_master(1)
        relay_y(0, 0, 0)
        take_half(0, 1, 1, w_in)
        t_z(0)
        z_pre(0, 1)
        t_z(1)
        relay_x(1, 0)
        relay_x(0, 1)
        mid_x(0, 1)
        mid_x(1, 0)
        end_x(0, 0)
        end_x(0, 1)
        z_pre(1, 0)
        mid_x(0, 0)
        far_y(0, 1)
        far_y(0, 0)
        z_pre(1, 1)
        relay_y(0, 1, 1)
        send_y(0, 1, 0)
        take_half(1, 1, 0, w_in)
        relay_y(0, 0, 1)
        relay_y(0, 1, 0)
        take_half(1, 1, 1, w_in)
        end_y(0, 0, 0)
        end_y(0, 1, 1)
        end_y(0, 0, 1)
        end_x(1, 0)
        wait_sib(0, 0)
        end_y(0, 1, 0)


    @when_not
    def _():
        send_y(0, 0, 0)
        t_z(0)
        send_y(0, 1, 0)
        relay_y(0, 0, 0)
        z_far(0, 1)
        z_in(0, 1)
        t_z(1)
        end_y(0, 0, 0)
        z_in(1, 1)
        take_half(0, 0, 0, w_far)
        far_y(0, 1)
        pass_on(0, 0)
        far_y(0, 0)
        relay_y(0, 1, 1)
        pass_on(0, 1)
        z_far(1, 0)
        take_half(0, 0, 1, w_far)
        relay_y(0, 0, 1)
        relay_x(0, 0)
        end_y(0, 1, 1)
        relay_y(0, 1, 0)
        z_far(1, 1)
        take_half(0, 1, 0, w_anti)
        end_x(0, 0)
        end_y(0, 1, 0)
        end_y(0, 0, 1)
        mid_x(0, 0)
        wait_sib(0, 1)
        z_in(1, 0)
        pass_on(1, 0)
        take_half(0, 1, 1, w_anti)

    away0()

    @when_master
    def _():
        wait_sib(0, 1)


    @when_not
    def _():
        wait_sib(0, 0)

    own0(zh)

    @when_master
    def _():
        relay_x(1, 1)


    @when_not
    def _():
        relay_x(0, 1)
        mid_x(0, 1)
        take_half(1, 0, 0, w_far)
        end_x(0, 1)
        pass_on(1, 1)
        take_half(1, 0, 1, w_far)

    own0(1 - zh)
    gate()

    @when_master
    def _():
        end_x(1, 1)
        far_y(1, 0)
        relay_y(1, 0, 0)
        relay_y(1, 1, 0)

    rim()

    @when_master
    def _():
        mid_x(1, 1)
        far_y(1, 1)
        end_y(1, 0, 0)
        relay_y(1, 2, 0)
        relay_y(1, 0, 1)
        end_y(1, 2, 0)
        far_y(1, 2)
        wait_sib(1, 0)
        relay_y(1, 1, 1)
        end_y(1, 1, 0)
        wait_sib(1, 1)


    @when_not
    def _():
        relay_x(1, 0)
        take_half(1, 1, 0, w_anti)
        relay_y(1, 0, 0)
        relay_y(1, 2, 0)
        take_half(1, 1, 1, w_anti)
        relay_y(1, 1, 0)
        end_x(1, 0)
        far_y(1, 0)
        relay_x(1, 1)
        end_y(1, 1, 0)
        mid_x(1, 1)
        far_y(1, 1)
        end_y(1, 0, 0)
        mid_x(1, 0)
        relay_y(1, 0, 1)
        relay_y(1, 1, 1)
        end_x(1, 1)
        far_y(1, 2)
        wait_sib(1, 1)
        wait_sib(1, 0)

    near2(0)

    @when_master
    def _():
        end_y(1, 0, 1)


    @when_not
    def _():
        end_y(1, 0, 1)

    far2(0)
    near2(1)

    @when_master
    def _():
        end_y(1, 1, 1)
        relay_y(1, 2, 1)


    @when_not
    def _():
        end_y(1, 1, 1)

    far2(1)

    @when_not
    def _():
        end_y(1, 2, 0)
        relay_y(1, 2, 1)

    near2(2)

    @when_master
    def _():
        end_y(1, 2, 1)


    @when_not
    def _():
        end_y(1, 2, 1)

    far2(2)
    result(2)
    result(0)
    result(1)

    def last(only):
        for name, roles in sent.items():
            if ("all" in roles or len(roles) == 2) == (only == "all") and (only == "all" or only in roles):
                senders[name[0]](*name[1:]).wait_send()

    last("all")

    @when_master
    def _():
        last("master")

    @when_not
    def _():
        last("nm")


COPIES = 144


def on_device(tokens, value_weight, key_gate, query_gate, conv_filter, out_weight):
    hbm = pl.BlockSpec(memory_space=pl.ANY)
    vmem = pl.BlockSpec(memory_space=pltpu.VMEM)
    bf16, f32 = jnp.bfloat16, jnp.float32
    return pl.pallas_call(
        kernel,
        out_shape=jax.ShapeDtypeStruct((ROWS, WIDTH), bf16),
        in_specs=[hbm, hbm, hbm, hbm, vmem, hbm],
        out_specs=vmem,
        scratch_shapes=[
            pltpu.VMEM((17, WIDTH, WIDTH), bf16),
            pltpu.VMEM((17, WIDTH, WIDTH), bf16),
            pltpu.VMEM((8, ROWS, WIDTH), bf16),
            pltpu.VMEM((8, ROWS, WIDTH), bf16),
            pltpu.VMEM((WIDTH // GROUP * TAPS, 2 * TAPS), bf16),
            pltpu.VMEM((WIDTH // GROUP, 2 * TAPS), f32),
            pltpu.VMEM((TAPS + ROWS, WIDTH), bf16),
            pltpu.VMEM((ROWS, WIDTH), bf16),
            pltpu.VMEM((ROWS, WIDTH), bf16),
            pltpu.VMEM((ROWS, WIDTH), f32),
            pltpu.VMEM((ROWS, WIDTH), f32),
            pltpu.VMEM((2, ROWS, WIDTH), bf16),
            pltpu.VMEM((2, ROWS, WIDTH), bf16),
            pltpu.SemaphoreType.DMA((COPIES,)),
            pltpu.SemaphoreType.DMA((COPIES,)),
            pltpu.SemaphoreType.DMA((5,)),
        ],
        compiler_params=pltpu.CompilerParams(
            collective_id=0, has_side_effects=True, vmem_limit_bytes=56 * 1024 * 1024
        ),
        cost_estimate=pl.CostEstimate(flops=6_442_450_944, bytes_accessed=3_000_000, transcendentals=0),
        name="hyena_block",
    )(tokens, value_weight, key_gate, query_gate, conv_filter, out_weight)


def solution(mesh):
    return jax.shard_map(
        on_device,
        mesh=mesh,
        in_specs=(
            P("tok", "ch"),
            P("tok", "ch"),
            P("tok", "ch"),
            P("tok", "ch"),
            P("ch", None),
            P("tok", "ch"),
        ),
        out_specs=P("tok", "ch"),
        check_vma=False,
    )
```

```python
import functools

import jax
import jax.numpy as jnp
from jax import lax
from jax.experimental import pallas as pl
from jax.experimental.pallas import tpu as pltpu
from jax.sharding import PartitionSpec as P

MESH = pl.DeviceIdType.MESH
TAPS = 128
GROUP = 16
ROWS = 384
WIDTH = 512
HALF = WIDTH // 2
RELAY = 16
CHUNKS = (((0, 192), (192, 192)), ((128, 128), (256, 128), (0, 128)))


class Names:
    def __init__(self):
        self.index = {}

    def __call__(self, name):
        return self.index.setdefault(name, len(self.index))


def place(x, y, z, c):
    return (x * 4 + (z // 4) * 2 + c, y * 4 + lax.rem(z, 4))


def kernel(
    tok_hbm, wv_hbm, key_hbm, query_hbm, filt_ref, wo_hbm,
    out_ref,
    wbuf_v, wbuf_o, tbuf_v, tbuf_o, band, base, ext, key, query,
    acc_away, acc_own, part_out, part_in, send_sem, recv_sem, local_sem,
):
    tok = lax.axis_index("tok")
    ch = lax.axis_index("ch")
    x, zh, c = tok // 4, lax.rem(tok // 2, 2), lax.rem(tok, 2)
    y, zl = ch // 4, lax.rem(ch, 4)
    zl1, zl0 = zl // 2, lax.rem(zl, 2)
    z = zh * 4 + zl
    master = c == zl0
    nm = jnp.logical_not(master)

    def near(zl0_):
        return zh * 4 + zl1 * 2 + zl0_

    xp, xm, x2 = lax.rem(x + 1, 4), lax.rem(x + 3, 4), lax.rem(x + 2, 4)
    yp, ym, y2 = lax.rem(y + 1, 4), lax.rem(y + 3, 4), lax.rem(y + 2, 4)
    dev_xp, dev_xm = place(xp, y, z, c), place(xm, y, z, c)
    dev_yp, dev_ym = place(x, yp, z, c), place(x, ym, z, c)
    dev_z1 = place(x, y, near(1 - zl0), c)
    dev_z2 = place(x, y, zh * 4 + (1 - zl1) * 2 + zl0, c)
    far_zl0 = jnp.where(master, zl0, 1 - zl0)
    dev_far = place(x, y, (1 - zh) * 4 + zl1 * 2 + far_zl0, jnp.where(master, c, 1 - c))
    dev_sib = place(x, y, z, 1 - c)
    dev_next = (lax.rem(tok + 1, 16), ch)
    dev_prev = (lax.rem(tok + 15, 16), ch)
    dev_other = (jnp.where(c == 1, lax.rem(tok + 1, 16), lax.rem(tok + 15, 16)), ch)

    barrier = pltpu.get_barrier_semaphore()
    partners = (dev_xp, dev_xm, dev_yp, dev_ym, dev_z1, dev_z2, dev_far, dev_sib, dev_other)
    for d in partners:
        pl.semaphore_signal(barrier, inc=1, device_id=d, device_id_type=MESH)
    pl.semaphore_wait(barrier, len(partners))

    w_hbm = (wv_hbm, wo_hbm)
    wbuf = (wbuf_v, wbuf_o)
    tbuf = (tbuf_v, tbuf_o)
    own, away = zl0, 1 - zl0
    names = Names()

    def slot(b, zz, j):
        return b * 8 + zz * 4 + j

    root_z = jnp.where(master, zh, 1 - zh)
    root_b = (jnp.where(master, own, away), jnp.where(master, away, own))

    sent = {}
    role = ["all"]

    class Sent:
        def __init__(self, name, src, dst, dev):
            i = names(name)
            self.name = name
            self.make = lambda: pltpu.make_async_remote_copy(
                src_ref=src, dst_ref=dst, send_sem=send_sem.at[i], recv_sem=recv_sem.at[i],
                device_id=dev, device_id_type=MESH,
            )

        def start(self):
            sent.setdefault(self.name, set()).add(role[0])
            self.make().start()

        def wait_recv(self):
            self.make().wait_recv()

        def wait_send(self):
            self.make().wait_send()

    copy = Sent

    def when_master(body):
        role[0] = "master"
        pl.when(master)(body)
        role[0] = "all"

    def when_not(body):
        role[0] = "nm"
        pl.when(nm)(body)
        role[0] = "all"

    def half(h):
        return pl.ds(h * HALF, HALF)

    def w_in(m, h, recv=False):
        s = slot(away if recv else own, zh, x)
        return copy(("in", m, h), w_hbm[m].at[half(h)], wbuf[m].at[s, half(h)], dev_z1)

    def w_far(m, h, recv=False):
        s = slot(away, 1 - zh, x) if recv else slot(own, zh, x)
        return copy(("far", m, h), w_hbm[m].at[half(h)], wbuf[m].at[s, half(h)], dev_far)

    def w_pre(m, h):
        return copy(("pre", m, h), w_hbm[m].at[half(h)], wbuf[m].at[RELAY, half(h)], dev_z1)

    def w_anti(m, h, recv=False):
        s = slot(own, 1 - zh, x) if recv else slot(away, zh, x)
        return copy(("anti", m, h), wbuf[m].at[RELAY, half(h)], wbuf[m].at[s, half(h)], dev_far)

    def w_x(m, r, way, h, recv=False, native=False):
        from_x = (xm if way > 0 else xp) if recv else x
        dst = wbuf[m].at[slot(root_b[r], root_z, from_x), half(h)]
        src = w_hbm[m].at[half(h)] if native else dst
        return copy(("x", m, r, way, h), src, dst, dev_xp if way > 0 else dev_xm)

    def w_fwd(m, r, way, recv=False):
        from_x = x2 if recv else (xm if way > 0 else xp)
        s = wbuf[m].at[slot(root_b[r], root_z, from_x), half(first_half(way))]
        return copy(("fwd", m, r, way), s, s, dev_xp if way > 0 else dev_xm)

    def w_sib(m, r, k, recv=False, native=False):
        j = (x, xm, xp, x2)[k]
        s = slot(1 - root_b[r], 1 - root_z, j) if recv else slot(root_b[r], root_z, j)
        src = w_hbm[m] if native else wbuf[m].at[s]
        return copy(("sib", m, r, k), src, wbuf[m].at[s], dev_sib)

    def first_half(way):
        return 0 if way > 0 else 1

    def t_y(q, ch_, p, way, h, recv=False):
        first, n = CHUNKS[q][ch_]
        from_y = (ym if way > 0 else yp) if recv else y
        k = (zl1 if p == 0 else 1 - zl1) * 4 + from_y
        rows = pl.ds(first + h * (n // 2), n // 2)
        ref = tbuf[q].at[k, rows]
        src = tok_hbm.at[rows] if q == 0 and p == 0 else ref
        return copy(("ty", q, ch_, p, way, h), src, ref, dev_yp if way > 0 else dev_ym)

    def t_fwd(q, ch_, p, way, recv=False):
        first, n = CHUNKS[q][ch_]
        from_y = y2 if recv else (ym if way > 0 else yp)
        k = (zl1 if p == 0 else 1 - zl1) * 4 + from_y
        ref = tbuf[q].at[k, pl.ds(first + first_half(way) * (n // 2), n // 2)]
        return copy(("tfwd", q, ch_, p, way), ref, ref, dev_yp if way > 0 else dev_ym)

    def t_far(q, ch_, recv=False):
        first, n = CHUNKS[q][ch_]
        ref = tbuf[q].at[((1 - zl1) if recv else zl1) * 4 + y, pl.ds(first, n)]
        src = tok_hbm.at[pl.ds(first, n)] if q == 0 else ref
        return copy(("tz", q, ch_), src, ref, dev_z2)

    def partial(q, ch_):
        rows = pl.ds(*CHUNKS[q][ch_])
        return copy(("c", q, ch_), part_out.at[q, rows], part_in.at[q, rows], dev_z1)

    def halo():
        return copy(("halo",), ext.at[pl.ds(ROWS, TAPS)], ext.at[pl.ds(0, TAPS)], dev_next)

    senders = {
        "in": w_in, "far": w_far, "pre": w_pre, "anti": w_anti, "x": w_x, "fwd": w_fwd, "sib": w_sib,
        "ty": t_y, "tfwd": t_fwd, "tz": t_far, "c": partial, "halo": halo,
    }

    def send_x(m, r, native=False):
        for h in range(2):
            for way in (1, -1):
                w_x(m, r, way, h if way > 0 else 1 - h, native=native).start()

    def relay_x(m, r):
        for way in (1, -1):
            w_x(m, r, way, first_half(way), recv=True).wait_recv()
            w_fwd(m, r, way).start()

    def mid_x(m, r):
        for way in (1, -1):
            w_x(m, r, way, 1 - first_half(way), recv=True).wait_recv()
        w_sib(m, r, 1).start()
        w_sib(m, r, 2).start()

    def end_x(m, r):
        for way in (1, -1):
            w_fwd(m, r, way, recv=True).wait_recv()
        w_sib(m, r, 3).start()

    def take_half(m, r, h, arrival):
        arrival(m, h, recv=True).wait_recv()
        for way in (1, -1):
            w_x(m, r, way, h).start()
        if h == 1:
            w_sib(m, r, 0).start()

    def send_y(q, ch_, p):
        for h in range(2):
            for way in (1, -1):
                t_y(q, ch_, p, way, h if way > 0 else 1 - h).start()

    def relay_y(q, ch_, p):
        for way in (1, -1):
            t_y(q, ch_, p, way, first_half(way), recv=True).wait_recv()
            t_fwd(q, ch_, p, way).start()

    def end_y(q, ch_, p):
        for way in (1, -1):
            t_y(q, ch_, p, way, 1 - first_half(way), recv=True).wait_recv()
            t_fwd(q, ch_, p, way, recv=True).wait_recv()

    def far_y(q, ch_):
        t_far(q, ch_, recv=True).wait_recv()
        send_y(q, ch_, 1)

    def z_in(m, h):
        w_in(m, h).start()

    def z_far(m, h):
        w_far(m, h).start()

    def z_pre(m, h):
        w_pre(m, h).start()

    def pass_on(m, h):
        w_pre(m, h).wait_recv()
        w_anti(m, h).start()

    def t_z(ch_):
        t_far(0, ch_).start()

    def x_master(m):
        send_x(m, 0, native=True)
        w_sib(m, 0, 0, native=True).start()

    def local(i, src, dst):
        return pltpu.make_async_copy(src, dst, local_sem.at[i])

    def own_w(m):
        return local(m, w_hbm[m], wbuf[m].at[slot(own, zh, x)])


    @when_not
    def _():
        z_far(0, 0)
        z_in(0, 0)


    @when_master
    def _():
        x_master(0)


    own_tok = local(2, tok_hbm, tbuf[0].at[zl1 * 4 + y])
    own_key = local(3, key_hbm, key)
    own_query = local(4, query_hbm, query)
    own_tok.start()
    own_key.start()
    own_query.start()

    @when_master
    def _():
        own_w(0).start()
        own_w(1).start()

    s_at = lax.broadcasted_iota(jnp.int32, (TAPS, 2 * TAPS), 1)
    j_at = lax.broadcasted_iota(jnp.int32, (TAPS, 2 * TAPS), 0)
    flip = jnp.where(s_at + j_at == TAPS, 1.0, 0.0).astype(jnp.bfloat16)
    base[...] = jnp.dot(filt_ref[...].astype(jnp.bfloat16), flip, preferred_element_type=jnp.float32)

    @pl.loop(0, WIDTH // GROUP)
    def _(g):
        rows = jnp.broadcast_to(base[pl.ds(g, 1), :], (TAPS, 2 * TAPS))
        turned = pltpu.roll(rows, 0, 1, stride=1, stride_axis=0)
        band[pl.ds(pl.multiple_of(g * TAPS, TAPS), TAPS), :] = turned.astype(jnp.bfloat16)

    acc_away[...] = jnp.zeros_like(acc_away)
    acc_own[...] = jnp.zeros_like(acc_own)

    def multiply(q, acc, rows, b, zz):
        for n in range(2):
            cols = pl.ds(n * 256, 256)
            total = None
            for j in range(4):
                term = jnp.dot(
                    tbuf[q][zz * 4 + j, rows, :],
                    wbuf[q][slot(b, zz, j), :, cols],
                    preferred_element_type=jnp.float32,
                )
                total = term if total is None else total + term
            acc[rows, cols] += total

    def wait_sib(m, r):
        for k in range(4):
            w_sib(m, r, k, recv=True).wait_recv()

    every = pl.ds(0, ROWS)
    k_own = zl1 * 4 + y

    def convolve(blocks):
        width = len(blocks) * TAPS
        lane_group = lax.rem(lax.broadcasted_iota(jnp.int32, (TAPS, width), 1), TAPS) // GROUP
        for tile in range(WIDTH // TAPS):
            lanes = pl.ds(tile * TAPS, TAPS)
            parts = [ext[pl.ds(block * TAPS, 2 * TAPS), lanes] for block in blocks]
            window = parts[0] if len(parts) == 1 else jnp.concatenate(parts, axis=1)
            conv = None
            for g in range(8):
                raw = jnp.dot(
                    band[pl.ds((tile * 8 + g) * TAPS, TAPS), :], window, preferred_element_type=jnp.float32
                )
                conv = raw if conv is None else jnp.where(lane_group == g, raw, conv)
            for i, block in enumerate(blocks):
                rows = pl.ds(block * TAPS, TAPS)
                shaped = conv[:, i * TAPS : (i + 1) * TAPS] * query[rows, lanes].astype(jnp.float32)
                tbuf_o[k_own, rows, lanes] = shaped.astype(jnp.bfloat16)

    def send_shaped(ch_):
        t_far(1, ch_).start()
        send_y(1, ch_, 0)

    def away0():
        own_tok.wait()

        @pl.when(master)
        def _():
            own_w(0).wait()
            own_w(1).wait()

        for ch_ in range(2):
            rows = pl.ds(*CHUNKS[0][ch_])
            for zz in range(2):
                multiply(0, acc_away, rows, away, zz)
            part_out[0, rows] = acc_away[rows].astype(jnp.bfloat16)
            partial(0, ch_).start()
        acc_away[...] = jnp.zeros_like(acc_away)

    def own0(zz):
        multiply(0, acc_own, every, own, zz)

    def gate():
        own_key.wait()
        own_query.wait()
        partial(0, 0).wait_recv()
        partial(0, 1).wait_recv()
        values = (acc_own[...] + part_in[0].astype(jnp.float32)).astype(jnp.bfloat16)
        ext[pl.ds(TAPS, ROWS), :] = (values.astype(jnp.float32) * key[...].astype(jnp.float32)).astype(jnp.bfloat16)
        halo().start()
        convolve((1,))
        send_shaped(0)
        convolve((2,))
        send_shaped(1)
        acc_own[...] = jnp.zeros_like(acc_own)

    def rim():
        halo().wait_recv()

        @pl.when(tok == 0)
        def _():
            ext[pl.ds(0, TAPS), :] = jnp.zeros((TAPS, WIDTH), jnp.bfloat16)

        convolve((0,))
        send_shaped(2)

    def near2(ch_):
        rows = pl.ds(*CHUNKS[1][ch_])
        multiply(1, acc_away, rows, away, zl1)
        multiply(1, acc_own, rows, own, zl1)

    def far2(ch_):
        rows = pl.ds(*CHUNKS[1][ch_])
        multiply(1, acc_away, rows, away, 1 - zl1)
        part_out[1, rows] = acc_away[rows].astype(jnp.bfloat16)
        partial(1, ch_).start()
        multiply(1, acc_own, rows, own, 1 - zl1)

    def result(ch_):
        rows = pl.ds(*CHUNKS[1][ch_])
        partial(1, ch_).wait_recv()
        out_ref[rows] = (acc_own[rows] + part_in[1, rows].astype(jnp.float32)).astype(jnp.bfloat16)


    @when_master
    def _():
        relay_x(0, 0)
        take_half(0, 1, 0, w_in)
        x_master(1)
        z_pre(0, 0)
        send_y(0, 0, 0)
        relay_y(0, 0, 0)
        take_half(0, 1, 1, w_in)
        t_z(0)
        relay_x(0, 1)
        z_pre(0, 1)
        t_z(1)
        relay_x(1, 0)
        end_y(0, 0, 0)
        z_pre(1, 0)
        far_y(0, 0)
        end_x(0, 0)
        far_y(0, 1)
        mid_x(0, 1)
        end_x(0, 1)
        z_pre(1, 1)
        relay_y(0, 1, 1)
        mid_x(0, 0)
        send_y(0, 1, 0)
        relay_y(0, 0, 1)
        end_y(0, 1, 1)
        take_half(1, 1, 0, w_in)
        mid_x(1, 0)
        relay_y(0, 1, 0)
        end_y(0, 0, 1)
        end_y(0, 1, 0)
        take_half(1, 1, 1, w_in)
        end_x(1, 0)
        wait_sib(0, 0)


    @when_not
    def _():
        z_far(0, 1)
        t_z(0)
        send_y(0, 0, 0)
        relay_y(0, 0, 0)
        z_in(0, 1)
        t_z(1)
        end_y(0, 0, 0)
        z_in(1, 1)
        far_y(0, 1)
        take_half(0, 0, 0, w_far)
        send_y(0, 1, 0)
        far_y(0, 0)
        pass_on(0, 0)
        pass_on(0, 1)
        take_half(0, 0, 1, w_far)
        relay_y(0, 1, 1)
        z_far(1, 0)
        relay_y(0, 0, 1)
        relay_x(0, 0)
        mid_x(0, 0)
        end_y(0, 1, 1)
        relay_y(0, 1, 0)
        take_half(0, 1, 0, w_anti)
        end_x(0, 0)
        end_y(0, 0, 1)
        z_in(1, 0)
        wait_sib(0, 1)
        end_y(0, 1, 0)
        take_half(0, 1, 1, w_anti)
        z_far(1, 1)

    away0()

    @when_master
    def _():
        wait_sib(0, 1)


    @when_not
    def _():
        wait_sib(0, 0)

    own0(zh)

    @when_master
    def _():
        relay_x(1, 1)


    @when_not
    def _():
        relay_x(0, 1)
        mid_x(0, 1)
        take_half(1, 0, 0, w_far)
        end_x(0, 1)
        pass_on(1, 1)
        take_half(1, 0, 1, w_far)
        pass_on(1, 0)

    own0(1 - zh)
    gate()

    @when_master
    def _():
        far_y(1, 0)
        mid_x(1, 1)
        end_x(1, 1)

    rim()

    @when_master
    def _():
        relay_y(1, 0, 0)
        relay_y(1, 1, 0)
        far_y(1, 1)
        relay_y(1, 0, 1)
        end_y(1, 0, 0)
        relay_y(1, 2, 0)
        relay_y(1, 1, 1)
        end_y(1, 2, 0)
        end_y(1, 1, 0)
        wait_sib(1, 0)
        far_y(1, 2)
        wait_sib(1, 1)


    @when_not
    def _():
        take_half(1, 1, 0, w_anti)
        relay_y(1, 0, 0)
        relay_x(1, 0)
        take_half(1, 1, 1, w_anti)
        relay_y(1, 1, 0)
        relay_y(1, 2, 0)
        far_y(1, 0)
        end_x(1, 0)
        relay_x(1, 1)
        mid_x(1, 1)
        end_y(1, 1, 0)
        end_y(1, 0, 0)
        far_y(1, 1)
        mid_x(1, 0)
        relay_y(1, 0, 1)
        wait_sib(1, 0)
        relay_y(1, 1, 1)
        far_y(1, 2)
        end_x(1, 1)
        wait_sib(1, 1)

    near2(0)

    @when_master
    def _():
        end_y(1, 0, 1)


    @when_not
    def _():
        end_y(1, 2, 0)

    near2(1)

    @when_not
    def _():
        end_y(1, 0, 1)

    far2(0)

    @when_master
    def _():
        end_y(1, 1, 1)
        relay_y(1, 2, 1)


    @when_not
    def _():
        end_y(1, 1, 1)

    far2(1)

    @when_not
    def _():
        relay_y(1, 2, 1)

    near2(2)

    @when_master
    def _():
        end_y(1, 2, 1)


    @when_not
    def _():
        end_y(1, 2, 1)

    far2(2)
    result(0)
    result(2)
    result(1)

    def last(only):
        for name, roles in sent.items():
            if ("all" in roles or len(roles) == 2) == (only == "all") and (only == "all" or only in roles):
                senders[name[0]](*name[1:]).wait_send()

    last("all")

    @when_master
    def _():
        last("master")

    @when_not
    def _():
        last("nm")


COPIES = 144


def on_device(tokens, value_weight, key_gate, query_gate, conv_filter, out_weight):
    hbm = pl.BlockSpec(memory_space=pl.ANY)
    vmem = pl.BlockSpec(memory_space=pltpu.VMEM)
    bf16, f32 = jnp.bfloat16, jnp.float32
    return pl.pallas_call(
        kernel,
        out_shape=jax.ShapeDtypeStruct((ROWS, WIDTH), bf16),
        in_specs=[hbm, hbm, hbm, hbm, vmem, hbm],
        out_specs=vmem,
        scratch_shapes=[
            pltpu.VMEM((17, WIDTH, WIDTH), bf16),
            pltpu.VMEM((17, WIDTH, WIDTH), bf16),
            pltpu.VMEM((8, ROWS, WIDTH), bf16),
            pltpu.VMEM((8, ROWS, WIDTH), bf16),
            pltpu.VMEM((WIDTH // GROUP * TAPS, 2 * TAPS), bf16),
            pltpu.VMEM((WIDTH // GROUP, 2 * TAPS), f32),
            pltpu.VMEM((TAPS + ROWS, WIDTH), bf16),
            pltpu.VMEM((ROWS, WIDTH), bf16),
            pltpu.VMEM((ROWS, WIDTH), bf16),
            pltpu.VMEM((ROWS, WIDTH), f32),
            pltpu.VMEM((ROWS, WIDTH), f32),
            pltpu.VMEM((2, ROWS, WIDTH), bf16),
            pltpu.VMEM((2, ROWS, WIDTH), bf16),
            pltpu.SemaphoreType.DMA((COPIES,)),
            pltpu.SemaphoreType.DMA((COPIES,)),
            pltpu.SemaphoreType.DMA((5,)),
        ],
        compiler_params=pltpu.CompilerParams(
            collective_id=0, has_side_effects=True, vmem_limit_bytes=56 * 1024 * 1024
        ),
        cost_estimate=pl.CostEstimate(flops=6_442_450_944, bytes_accessed=3_000_000, transcendentals=0),
        name="hyena_block",
    )(tokens, value_weight, key_gate, query_gate, conv_filter, out_weight)


def solution(mesh):
    return jax.shard_map(
        on_device,
        mesh=mesh,
        in_specs=(
            P("tok", "ch"),
            P("tok", "ch"),
            P("tok", "ch"),
            P("tok", "ch"),
            P("ch", None),
            P("tok", "ch"),
        ),
        out_specs=P("tok", "ch"),
        check_vma=False,
    )
```
